32 devices in a mesh: dp: 4 (over z), tensor: 8 (over y, x, core).
Axes of the slice: x: 2, y: 2, z: 4, core: 2. Of those that a mesh axis runs over, the one named last changes fastest.
Arguments:
- queries: bfloat16 [512, 8192], P('dp', 'tensor'), may hold values from -6 to 6
- keys: bfloat16 [512, 8192], P('dp', 'tensor'), may hold values from -6 to 6
- values: bfloat16 [512, 8192], P('dp', 'tensor'), may hold values from -6 to 6
- doc_start: int32 [512], P('dp'), may hold values from 0 to 511, as said below
- filters: float32 [512, 128], P('tensor'), may hold values from -0.5 to 0.5
- out_weight: bfloat16 [8192, 8192], P('tensor'), may hold values from -0.09375 to 0.09375
- out_grad: bfloat16 [512, 8192], P('dp'), may hold values from -6 to 6
Outputs:
- output: bfloat16 [512, 8192], P('dp', 'tensor')
- q_grad: bfloat16 [512, 8192], P('dp', 'tensor')
- k_grad: bfloat16 [512, 8192], P('dp', 'tensor')
- v_grad: bfloat16 [512, 8192], P('dp', 'tensor')
- filter_grad: float32 [512, 128], P('tensor')
The draws below stay inside these ranges and needn't reach their ends.
Inputs may be any that keep to these rules, and one draw needn't show every extreme that they name: doc_start[0] = 0; for t > 0, doc_start[t] is t (a document begins) or doc_start[t - 1]; the last position begins a document.
All inputs are finite; a program needn't handle non-finite values.
Results may differ from the reference program's by a relative error of at most 0.015.
Values may be sent and summed in bfloat16 or wider, within the bound.
No kernel may reach another device: no remote copies, remote signals or barrier semaphores. Data moves between devices by JAX's collectives and lax.ppermute only.
A program may use at most 128 MiB of HBM per device.

```python
import jax
import jax.numpy as jnp
from jax import lax

D = 8192
TAPS = 128
GROUP = 16
SEQ = 512
FILTERS = 512
N_TENSOR = 8


def draw_doc_start(key, part):
    places = jnp.arange(SEQ, dtype=jnp.int32)
    marks = jax.random.randint(key, (SEQ,), 0, 700)
    starts = jnp.where((marks == 0) | (places == 0) | (places == SEQ - 1), places, 0)
    return lax.cummax(starts, axis=0).astype(jnp.int32)


def strengthened(entries, stream_key, source, target, blocks, factor):
    owner, partner = [(jnp.arange(entries.shape[dim]) // (entries.shape[dim] // blocks)).reshape([-1 if axis == dim else 1 for axis in range(entries.ndim)]) for dim in (source, target)]
    chosen = jax.random.permutation(stream_key, blocks)[partner]
    strong = (owner == chosen) | (owner == (partner + blocks // 2) % blocks)
    return jnp.where(strong, factor * entries, entries)


def block_scale(rng, extent, split, smallest, largest):
    gain = 1.0
    for dim, shards_of in split:
        steps = jax.random.uniform(jax.random.fold_in(jax.random.fold_in(rng, 6), dim), (shards_of,), jnp.float32, smallest / len(split), largest / len(split))
        gain = gain * jnp.repeat(jnp.exp(steps), extent[dim] // shards_of).reshape((-1,) + (1,) * (len(extent) - 1 - dim))
    return gain


def centred(own_key, dims, scale, limit, shards=(), kind=jnp.bfloat16):
    factor_of = block_scale(own_key, dims, shards, -0.22, 0.18) if shards else 1.0
    entries = jax.random.normal(own_key, dims, jnp.float32) * scale * factor_of
    return jnp.minimum(jnp.maximum(entries, -limit), limit).astype(kind)


def gaussian_with(own_key, dims, deviation, most, pieces, heavy, kind=jnp.bfloat16):
    entries = deviation * jax.random.normal(own_key, dims, jnp.float32)
    if pieces:
        entries = entries * block_scale(own_key, dims, pieces, -0.22, 0.18)
    return jnp.clip(strengthened(entries, jax.random.fold_in(own_key, 3), *heavy), -most, most).astype(kind)


def setup_inputs(seed: int = 0) -> dict:
    key_list = jax.random.split(jax.random.key(seed), 8)
    queries = centred(key_list[0], (SEQ, D), 1.0, 6.0, ((0, 4), (1, 8)))
    keys = centred(key_list[1], (SEQ, D), 1.0, 6.0, ((0, 4), (1, 8)))
    values = centred(key_list[2], (SEQ, D), 1.0, 6.0, ((0, 4), (1, 8)))
    doc_start = draw_doc_start(jax.random.fold_in(key_list[7], 71), 0)
    filters = centred(key_list[4], (FILTERS, TAPS), TAPS ** -0.5, 0.5, ((0, 8),), jnp.float32)
    out_weight = gaussian_with(key_list[5], (D, D), D ** -0.5, 0.09375, ((0, 8),), (0, 1, 8, 2.0))
    out_grad = centred(key_list[6], (SEQ, D), 1.0, 6.0, ((0, 4),))
    return {"queries": queries, "keys": keys, "values": values, "doc_start": doc_start, "filters": filters, "out_weight": out_weight, "out_grad": out_grad}


def forward_conv(field, chan_filt, doc_start):
    seq_len, width = field.shape
    taps = chan_filt.shape[1]
    position = jnp.arange(seq_len, dtype=jnp.int32)
    padded = jnp.concatenate([jnp.zeros((taps - 1, width), jnp.float32), field], axis=0)

    def step(tap, total):
        shifted = lax.dynamic_slice_in_dim(padded, (taps - 1 - tap).astype(jnp.int32), seq_len, 0)
        column = lax.dynamic_slice_in_dim(chan_filt, tap.astype(jnp.int32), 1, 1)[:, 0]
        valid = (position - tap >= doc_start)[:, None]
        return total + jnp.where(valid, shifted * column[None, :], 0.0)

    return lax.fori_loop(0, taps, step, jnp.zeros((seq_len, width), jnp.float32))


def backward_conv(grad, chan_filt, doc_start):
    seq_len, width = grad.shape
    taps = chan_filt.shape[1]
    position = jnp.arange(seq_len, dtype=jnp.int32)
    padded = jnp.concatenate([grad, jnp.zeros((taps - 1, width), jnp.float32)], axis=0)
    doc_pad = jnp.concatenate([doc_start, jnp.full((taps - 1,), seq_len, jnp.int32)], axis=0)

    def step(tap, total):
        shifted = lax.dynamic_slice_in_dim(padded, tap.astype(jnp.int32), seq_len, 0)
        docs = lax.dynamic_slice_in_dim(doc_pad, tap.astype(jnp.int32), seq_len, 0)
        column = lax.dynamic_slice_in_dim(chan_filt, tap.astype(jnp.int32), 1, 1)[:, 0]
        valid = (position >= docs)[:, None]
        return total + jnp.where(valid, shifted * column[None, :], 0.0)

    return lax.fori_loop(0, taps, step, jnp.zeros((seq_len, width), jnp.float32))


def filter_terms(grad, field, doc_start, groups):
    seq_len, width = field.shape
    taps = TAPS
    position = jnp.arange(seq_len, dtype=jnp.int32)
    padded = jnp.concatenate([jnp.zeros((taps - 1, width), jnp.float32), field], axis=0)

    def step(tap, total):
        shifted = lax.dynamic_slice_in_dim(padded, (taps - 1 - tap).astype(jnp.int32), seq_len, 0)
        valid = (position - tap >= doc_start)[:, None]
        per_chan = jnp.sum(jnp.where(valid, grad * shifted, 0.0), axis=0)
        per_group = jnp.sum(per_chan.reshape(groups, width // groups), axis=1)
        return lax.dynamic_update_slice(total, per_group[:, None], (jnp.int32(0), tap.astype(jnp.int32)))

    return lax.fori_loop(0, taps, step, jnp.zeros((groups, taps), jnp.float32))


def reference(queries, keys, values, doc_start, filters, out_weight, out_grad):
    groups = filters.shape[0]
    chan_filt = jnp.repeat(filters, GROUP, axis=0)
    mixed = (keys.astype(jnp.float32) * values.astype(jnp.float32)).astype(jnp.bfloat16)
    mixed_f = mixed.astype(jnp.float32)
    conv = forward_conv(mixed_f, chan_filt, doc_start)
    gated = (queries.astype(jnp.float32) * conv).astype(jnp.bfloat16)
    block = D // N_TENSOR

    def project(index, total):
        gated_block = lax.dynamic_slice_in_dim(gated, (index * block).astype(jnp.int32), block, 1)
        weight_block = lax.dynamic_slice_in_dim(out_weight, (index * block).astype(jnp.int32), block, 0)
        part = jnp.dot(gated_block, weight_block, preferred_element_type=jnp.float32)
        return total + lax.optimization_barrier(part.astype(jnp.bfloat16)).astype(jnp.float32)

    summed = lax.fori_loop(0, N_TENSOR, project, jnp.zeros((SEQ, D), jnp.float32))
    output = summed.astype(jnp.bfloat16)
    gated_grad = jnp.dot(out_grad, out_weight.T, preferred_element_type=jnp.float32)
    q_grad = (gated_grad * conv).astype(jnp.bfloat16)
    conv_grad = (gated_grad * queries.astype(jnp.float32)).astype(jnp.bfloat16)
    conv_grad_f = conv_grad.astype(jnp.float32)
    mixed_grad = backward_conv(conv_grad_f, chan_filt, doc_start)
    k_grad = (mixed_grad * values.astype(jnp.float32)).astype(jnp.bfloat16)
    v_grad = (mixed_grad * keys.astype(jnp.float32)).astype(jnp.bfloat16)
    scale = jnp.float32((SEQ * GROUP) ** -0.5)
    filter_grad = filter_terms(conv_grad_f, mixed_f, doc_start, groups) * scale
    return output, q_grad, k_grad, v_grad, filter_grad
```

```python
import functools

import jax
import jax.numpy as jnp
from jax import lax
from jax.experimental import pallas as pl
from jax.experimental.pallas import tpu as pltpu
from jax.sharding import PartitionSpec as P

F32, BF16 = jnp.float32, jnp.bfloat16
LANES = 128
SUBLANES = 8
NT = (((1,), (1,)), ((), ()))
VMEM = pl.BlockSpec(memory_space=pltpu.VMEM)
MIB = 1 << 20


def call(body, operands, outs, name, scratch=(), held=None):
    shapes = [jax.ShapeDtypeStruct(*s) for s in outs]
    aliases = {}
    if held is not None:
        operands = [held_in_vmem(v) if k == held else v for k, v in enumerate(operands)]
        shapes = [pltpu.VMEM(operands[held].shape, operands[held].dtype)] + shapes
        aliases = {held: 0}
    return pl.pallas_call(
        body,
        out_shape=shapes,
        in_specs=[VMEM] * len(operands),
        out_specs=[VMEM] * len(shapes),
        input_output_aliases=aliases,
        scratch_shapes=list(scratch),
        compiler_params=pltpu.CompilerParams(vmem_limit_bytes=16 * MIB),
        name=name,
    )(*operands)


def held_in_vmem(value):
    return pltpu.with_memory_space_constraint(value, pltpu.VMEM)


def mirror(taps):
    i = lax.broadcasted_iota(jnp.int32, (taps, taps), 0)
    j = lax.broadcasted_iota(jnp.int32, (taps, taps), 1)
    return (i + j == taps) | ((i == 0) & (j == 0))


def doc_offsets(doc_ref, taps):
    first = lax.axis_index("dp") * taps
    lane = jnp.broadcast_to((doc_ref[...] - first).astype(F32), (taps, taps))
    return lane, lane.T


def grid_of(taps):
    return (
        lax.broadcasted_iota(jnp.int32, (taps, taps), 0).astype(F32),
        lax.broadcasted_iota(jnp.int32, (taps, taps), 1).astype(F32),
    )


def row_masks(doc_ref, taps):
    _, doc = doc_offsets(doc_ref, taps)
    t, s = grid_of(taps)
    return (s <= t) & (s >= doc), (s > t) & (s - taps >= doc)


def column_masks(doc_ref, taps):
    doc, _ = doc_offsets(doc_ref, taps)
    s, t = grid_of(taps)
    return (s <= t) & (s >= doc), (s > t) & (s >= doc[:, taps - 1 :])


def front_body(chunks, doc_ref, filt_ref, grad_ref, weight_ref, queries_ref,
               fwd_ref, bwd_ref, gated_ref, conv_ref, lead_ref, held_ref, turned, arrived):
    groups, taps = filt_ref.shape
    step = weight_ref.shape[0] // chunks
    copies = [
        pltpu.make_async_copy(weight_ref.at[pl.ds(k * step, step)], held_ref.at[pl.ds(k * step, step)], arrived.at[k])
        for k in range(chunks)
    ]
    for copy in copies:
        copy.start()
    turned[...] = jnp.dot(
        filt_ref[...].astype(BF16), mirror(taps).astype(BF16), preferred_element_type=F32
    )
    here, before = [m.astype(BF16) for m in row_masks(doc_ref, taps)]
    here_t, after = [m.astype(BF16) for m in column_masks(doc_ref, taps)]

    @pl.loop(0, groups, unroll=16)
    def _(g):
        rows = pl.ds(pl.multiple_of(g * taps, taps), taps)

        def circulant(ref):
            line = jnp.broadcast_to(ref[pl.ds(g, 1), :], (taps, taps))
            return pltpu.roll(line, 0, 1, stride=1, stride_axis=0).astype(BF16)

        fwd = circulant(turned)
        fwd_ref[rows, :taps] = fwd * here
        fwd_ref[rows, taps:] = fwd * before
        bwd = circulant(filt_ref)
        bwd_ref[rows, :taps] = bwd * here_t
        bwd_ref[rows, taps:] = bwd * after

    _, doc = doc_offsets(doc_ref, taps)
    for k, copy in enumerate(copies):
        copy.wait()
        columns = pl.ds(k * step, step)
        total = lax.dot_general(grad_ref[...], held_ref[columns, :], NT, preferred_element_type=F32)
        gated_ref[:, columns] = total
        conv_grad = (total * queries_ref[:, columns].astype(F32)).astype(BF16)
        conv_ref[:, columns] = conv_grad
        lead_ref[:, columns] = jnp.where(doc[:, :1] < 0, conv_grad, jnp.zeros_like(conv_grad))


def filtered(band_ref, near_ref, far_ref, columns, member):
    taps = near_ref.shape[0]
    groups = LANES // member
    both = jnp.concatenate([near_ref[:, columns], far_ref[:, columns]], axis=0)
    bands = pl.ds(columns.start // LANES * groups * taps, groups * taps)
    every = jnp.dot(band_ref[bands, :], both, preferred_element_type=F32)
    owner = lax.div(lax.broadcasted_iota(jnp.int32, (taps, LANES), 1), member)
    total = every[:taps]
    for g in range(1, groups):
        total = jnp.where(owner == g, every[g * taps : (g + 1) * taps], total)
    return total


def block_columns(offset, sibling, width):
    me = lax.axis_index("tensor")
    chip, core = lax.div(me, 2), lax.rem(me, 2)
    owner = 2 * jnp.bitwise_xor(chip, offset) + (1 - core if sibling else core)
    return pl.ds(pl.multiple_of(owner * width, width), width)


def conv_body(member, offsets, band_ref, mixed_ref, before_ref, queries_ref, weight_ref, held_ref, conv_ref, gated_ref, *part_refs):
    chan = mixed_ref.shape[1]

    for tile in range(chan // LANES):
        columns = pl.ds(tile * LANES, LANES)
        conv = filtered(band_ref, mixed_ref, before_ref, columns, member)
        conv_ref[:, columns] = conv
        gated_ref[:, columns] = (queries_ref[:, columns].astype(F32) * conv).astype(BF16)

    part_body(offsets, True, weight_ref, gated_ref, held_ref, *part_refs)


def part_body(offsets, sibling, weight_ref, gated_ref, *refs):
    count = len(offsets)
    adds, outs = refs[: -1 - count], refs[-count:]
    for k, offset in enumerate(offsets):
        columns = block_columns(offset, sibling, outs[k].shape[1])
        part = jnp.dot(gated_ref[...], weight_ref[:, columns], preferred_element_type=F32)
        if adds:
            part = part.astype(BF16).astype(F32) + adds[k][...].astype(F32)
        outs[k][...] = part.astype(BF16)


def filter_grad_body(member, scale, doc_ref, grad_ref, mixed_ref, before_ref, out_ref, sums):
    taps, chan = grad_ref.shape
    groups = LANES // member
    here, before = [m.astype(F32) for m in row_masks(doc_ref, taps)]
    owner = lax.div(lax.broadcasted_iota(jnp.int32, (taps, LANES), 1), member)

    for tile in range(chan // LANES):
        columns = pl.ds(tile * LANES, LANES)
        both = jnp.concatenate([mixed_ref[:, columns], before_ref[:, columns]], axis=0)
        grad = grad_ref[:, columns]
        apart = jnp.concatenate([grad * (owner == g).astype(BF16) for g in range(groups)], axis=0)
        every = lax.dot_general(apart, both, NT, preferred_element_type=F32)
        for g in range(groups):
            one = every[g * taps : (g + 1) * taps]
            one = one[:, :taps] * here + one[:, taps:] * before
            total = one[:SUBLANES]
            for b in range(SUBLANES, taps, SUBLANES):
                total = total + pltpu.roll(one[b : b + SUBLANES], taps - b, 1)
            sums[tile * groups + g] = total

    total = sums[:, 0, :]
    for i in range(1, SUBLANES):
        total = total + pltpu.roll(sums[:, i, :], taps - i, 1)
    out_ref[...] = scale * jnp.dot(
        total, mirror(taps).astype(F32), precision=lax.Precision.HIGHEST, preferred_element_type=F32
    )


def input_grads_body(member, band_ref, grad_ref, after_ref, keys_ref, values_ref, gated_ref, conv_ref, q_ref, k_ref, v_ref):
    chan = grad_ref.shape[1]

    for tile in range(chan // LANES):
        columns = pl.ds(tile * LANES, LANES)
        mixed_grad = filtered(band_ref, grad_ref, after_ref, columns, member)
        k_ref[:, columns] = (mixed_grad * values_ref[:, columns].astype(F32)).astype(BF16)
        v_ref[:, columns] = (mixed_grad * keys_ref[:, columns].astype(F32)).astype(BF16)
        q_ref[:, columns] = (gated_ref[:, columns] * conv_ref[:, columns]).astype(BF16)


def shift(value, axis, by):
    devices = lax.axis_size(axis)
    return lax.ppermute(value, axis, [(i, i + by) for i in range(devices) if 0 <= i + by < devices])


def swap(value, mask):
    devices = lax.axis_size("tensor")
    return lax.ppermute(value, "tensor", [(i, i ^ mask) for i in range(devices)])


def summed_over_dp(terms):
    devices = lax.axis_size("dp")
    if devices > 4:
        return lax.psum(terms, "dp")
    total = terms
    for by in range(1, devices):
        total = total + lax.ppermute(terms, "dp", [(i, (i + by) % devices) for i in range(devices)])
    return total


def on_device(queries, keys, values, doc_start, filters, out_weight, out_grad):
    rows, chan = queries.shape
    groups, taps = filters.shape
    member = chan // groups
    n = lax.axis_size("tensor")
    width = out_weight.shape[1] // n
    assert rows == taps == LANES and LANES % member == 0
    doc = doc_start.reshape(1, rows)
    tile, tile32, block = ((rows, chan), BF16), ((rows, chan), F32), ((rows, width), BF16)
    bands = pltpu.VMEM((groups * taps, 2 * taps), BF16)

    mixed = (keys.astype(F32) * values.astype(F32)).astype(BF16)
    before = shift(mixed, "dp", 1)
    chunks = max(1, chan // LANES)
    fwd, bwd, gated_grad, conv_grad, leading, weight = pl.pallas_call(
        functools.partial(front_body, chunks),
        out_shape=[bands, bands] + [jax.ShapeDtypeStruct(*s) for s in (tile32, tile, tile)] + [pltpu.VMEM(out_weight.shape, BF16)],
        in_specs=[VMEM, VMEM, VMEM, pl.BlockSpec(memory_space=pl.ANY), VMEM],
        out_specs=[VMEM] * 6,
        scratch_shapes=[pltpu.VMEM((groups, taps), F32), pltpu.SemaphoreType.DMA((chunks,))],
        compiler_params=pltpu.CompilerParams(vmem_limit_bytes=16 * MIB),
        name="front",
    )(doc, filters, out_grad, out_weight, queries)
    fwd, bwd = held_in_vmem(fwd), held_in_vmem(bwd)

    if n == 8:
        some, rest = (3, 1), (2, 0)
        weight, conv, gated, *first = call(
            functools.partial(conv_body, member, some), (fwd, mixed, before, queries, weight),
            [tile32, tile, block, block], "conv", held=4,
        )
        first = [swap(v, 1) for v in first]
        weight, *second = call(
            functools.partial(part_body, rest, True), (weight, gated), [block, block], "part_rest", held=0
        )
        second = [swap(v, 1) for v in second]
        weight, far, near_x = call(
            functools.partial(part_body, some, False), (weight, gated, *first), [block, block], "sum_some", held=0
        )
        far, near_x = swap(far, 6), swap(near_x, 2)
        weight, near_y, own = call(
            functools.partial(part_body, rest, False), (weight, gated, *second), [block, block], "sum_rest", held=0
        )
        near_y, leading, conv_grad = lax.optimization_barrier((near_y, leading, conv_grad))
        near_y = swap(near_y, 4)
        output = sum(v.astype(F32) for v in (own, near_x, near_y, far)).astype(BF16)
    else:
        weight, conv, gated = call(
            functools.partial(conv_body, member, ()), (fwd, mixed, before, queries, weight), [tile32, tile], "conv", held=4
        )
        partial_out = jnp.dot(gated, out_weight, preferred_element_type=F32).astype(BF16)
        output = lax.psum_scatter(partial_out, "tensor", scatter_dimension=1, tiled=True)
    after = shift(leading, "dp", -1)
    scale = (rows * lax.axis_size("dp") * member) ** (-0.5)
    (terms,) = call(
        functools.partial(filter_grad_body, member, scale), (doc, conv_grad, mixed, before),
        [((groups, taps), F32)], "filter_grad", scratch=[pltpu.VMEM((groups, SUBLANES, taps), F32)],
    )
    filter_grad = summed_over_dp(terms)
    q_grad, k_grad, v_grad = call(
        functools.partial(input_grads_body, member), (bwd, conv_grad, after, keys, values, gated_grad, conv),
        [tile, tile, tile], "input_grads",
    )
    return (output, q_grad, k_grad, v_grad, filter_grad)


def solution(mesh):
    split = P("dp", "tensor")
    return jax.shard_map(
        on_device,
        mesh=mesh,
        in_specs=(split, split, split, P("dp"), P("tensor", None), P("tensor", None), P("dp", None)),
        out_specs=(split, split, split, split, P("tensor", None)),
        check_vma=False,
    )
```

```python
import functools

import jax
import jax.numpy as jnp
from jax import lax
from jax.experimental import pallas as pl
from jax.experimental.pallas import tpu as pltpu
from jax.sharding import PartitionSpec as P

F32, BF16 = jnp.float32, jnp.bfloat16
LANES = 128
SUBLANES = 8
NT = (((1,), (1,)), ((), ()))
VMEM = pl.BlockSpec(memory_space=pltpu.VMEM)
MIB = 1 << 20


def cost(us):
    return pl.CostEstimate(flops=int(us * 1.1e9), bytes_accessed=int(us * 3.6e6), transcendentals=0)


def call(body, operands, outs, name, us, scratch=(), held=None):
    shapes = [jax.ShapeDtypeStruct(*s) for s in outs]
    aliases = {}
    if held is not None:
        operands = [held_in_vmem(v) if k == held else v for k, v in enumerate(operands)]
        shapes = [pltpu.VMEM(operands[held].shape, operands[held].dtype)] + shapes
        aliases = {held: 0}
    return pl.pallas_call(
        body,
        out_shape=shapes,
        in_specs=[VMEM] * len(operands),
        out_specs=[VMEM] * len(shapes),
        input_output_aliases=aliases,
        scratch_shapes=list(scratch),
        compiler_params=pltpu.CompilerParams(vmem_limit_bytes=16 * MIB),
        cost_estimate=cost(us),
        name=name,
    )(*operands)


def held_in_vmem(value):
    return pltpu.with_memory_space_constraint(value, pltpu.VMEM)


def mirror(taps):
    i = lax.broadcasted_iota(jnp.int32, (taps, taps), 0)
    j = lax.broadcasted_iota(jnp.int32, (taps, taps), 1)
    return (i + j == taps) | ((i == 0) & (j == 0))


def doc_offsets(doc_ref, taps):
    first = lax.axis_index("dp") * taps
    lane = jnp.broadcast_to((doc_ref[...] - first).astype(F32), (taps, taps))
    return lane, lane.T


def grid_of(taps):
    return (
        lax.broadcasted_iota(jnp.int32, (taps, taps), 0).astype(F32),
        lax.broadcasted_iota(jnp.int32, (taps, taps), 1).astype(F32),
    )


def row_masks(doc_ref, taps):
    _, doc = doc_offsets(doc_ref, taps)
    t, s = grid_of(taps)
    return (s <= t) & (s >= doc), (s > t) & (s - taps >= doc)


def column_masks(doc_ref, taps):
    doc, _ = doc_offsets(doc_ref, taps)
    s, t = grid_of(taps)
    return (s <= t) & (s >= doc), (s > t) & (s >= doc[:, taps - 1 :])


def front_body(ahead, doc_hbm, filt_hbm, grad_hbm, weight_hbm, queries_hbm, fwd_ref, bwd_ref, gated_ref, conv_ref,
               lead_ref, weight_ref, doc_ref, filt_ref, turned, grad_ref, grad_t, queries_ref, arrived, came):
    groups, taps = filt_ref.shape
    chan = weight_ref.shape[0]
    step = min(2 * LANES, chan)
    count = chan // step
    share = -(-groups // count)
    small = [
        pltpu.make_async_copy(src, dst, came.at[k])
        for k, (src, dst) in enumerate(
            ((doc_hbm, doc_ref), (filt_hbm, filt_ref), (grad_hbm, grad_ref), (queries_hbm, queries_ref))
        )
    ]
    large = [
        pltpu.make_async_copy(weight_hbm.at[pl.ds(k * step, step)], weight_ref.at[pl.ds(k * step, step)], arrived.at[k])
        for k in range(count)
    ]
    for copy in small + large[:ahead]:
        copy.start()
    small[0].wait()
    here, before = [m.astype(BF16) for m in row_masks(doc_ref, taps)]
    here_t, after = [m.astype(BF16) for m in column_masks(doc_ref, taps)]
    _, doc = doc_offsets(doc_ref, taps)
    small[1].wait()
    turned[...] = jnp.dot(filt_ref[...].astype(BF16), mirror(taps).astype(BF16), preferred_element_type=F32)

    def circulant(ref, g):
        line = jnp.broadcast_to(ref[pl.ds(g, 1), :], (taps, taps))
        return pltpu.roll(line, 0, 1, stride=1, stride_axis=0).astype(BF16)

    for k in range(count):
        for g in range(k * share, min(groups, (k + 1) * share)):
            rows = pl.ds(g * taps, taps)
            fwd = circulant(turned, g)
            fwd_ref[rows, :taps] = fwd * here
            fwd_ref[rows, taps:] = fwd * before
            bwd = circulant(filt_ref, g)
            bwd_ref[rows, :taps] = bwd * here_t
            bwd_ref[rows, taps:] = bwd * after
        if k == 0:
            small[2].wait()
            for c in range(0, grad_ref.shape[1], LANES):
                grad_t[pl.ds(c, LANES), :] = grad_ref[:, pl.ds(c, LANES)].T
            small[3].wait()
        large[k].wait()
        if k + ahead < count:
            large[k + ahead].start()
        columns = pl.ds(k * step, step)
        total = jnp.dot(weight_ref[columns, :], grad_t[...], preferred_element_type=F32).T
        gated_ref[:, columns] = total
        conv_grad = (total * queries_ref[:, columns].astype(F32)).astype(BF16)
        conv_ref[:, columns] = conv_grad
        lead_ref[:, columns] = jnp.where(doc[:, :1] < 0, conv_grad, jnp.zeros_like(conv_grad))


def filtered(band_ref, near_ref, far_ref, columns, member):
    taps = near_ref.shape[0]
    groups = LANES // member
    both = jnp.concatenate([near_ref[:, columns], far_ref[:, columns]], axis=0)
    bands = pl.ds(columns.start // LANES * groups * taps, groups * taps)
    every = jnp.dot(band_ref[bands, :], both, preferred_element_type=F32)
    owner = lax.div(lax.broadcasted_iota(jnp.int32, (taps, LANES), 1), member)
    total = every[:taps]
    for g in range(1, groups):
        total = jnp.where(owner == g, every[g * taps : (g + 1) * taps], total)
    return total


def block_columns(offset, sibling, width):
    me = lax.axis_index("tensor")
    chip, core = lax.div(me, 2), lax.rem(me, 2)
    owner = 2 * jnp.bitwise_xor(chip, offset) + (1 - core if sibling else core)
    return pl.ds(pl.multiple_of(owner * width, width), width)


def conv_body(member, offsets, band_ref, mixed_ref, before_ref, queries_ref, weight_ref, held_ref, conv_ref, gated_ref, *part_refs):
    chan = mixed_ref.shape[1]

    for tile in range(chan // LANES):
        columns = pl.ds(tile * LANES, LANES)
        conv = filtered(band_ref, mixed_ref, before_ref, columns, member)
        conv_ref[:, columns] = conv
        gated_ref[:, columns] = (queries_ref[:, columns].astype(F32) * conv).astype(BF16)

    part_body(offsets, True, weight_ref, gated_ref, held_ref, *part_refs)


def part_body(offsets, sibling, weight_ref, gated_ref, *refs):
    rows = gated_ref.shape[0]
    for k, offset in enumerate(offsets):
        width = refs[-1].shape[1]
        stacked = pl.ds(k * rows, rows)
        columns = block_columns(offset, sibling, width)
        part = jnp.dot(gated_ref[...], weight_ref[:, columns], preferred_element_type=F32)
        if sibling:
            refs[-1][stacked, :] = part.astype(BF16)
        else:
            summed = part.astype(BF16).astype(F32) + refs[0][stacked, :].astype(F32)
            refs[k - len(offsets)][...] = summed.astype(BF16)


def filter_grad_body(member, scale, doc_ref, grad_ref, mixed_ref, before_ref, out_ref, sums):
    taps, chan = grad_ref.shape
    groups = LANES // member
    here, before = [m.astype(F32) for m in row_masks(doc_ref, taps)]
    owner = lax.div(lax.broadcasted_iota(jnp.int32, (taps, LANES), 1), member)

    for tile in range(chan // LANES):
        columns = pl.ds(tile * LANES, LANES)
        both = jnp.concatenate([mixed_ref[:, columns], before_ref[:, columns]], axis=0)
        grad = grad_ref[:, columns]
        apart = jnp.concatenate([grad * (owner == g).astype(BF16) for g in range(groups)], axis=0)
        every = lax.dot_general(apart, both, NT, preferred_element_type=F32)
        for g in range(groups):
            one = every[g * taps : (g + 1) * taps]
            one = one[:, :taps] * here + one[:, taps:] * before
            total = one[:SUBLANES]
            for b in range(SUBLANES, taps, SUBLANES):
                total = total + pltpu.roll(one[b : b + SUBLANES], taps - b, 1)
            sums[tile * groups + g] = total

    total = sums[:, 0, :]
    for i in range(1, SUBLANES):
        total = total + pltpu.roll(sums[:, i, :], taps - i, 1)
    out_ref[...] = scale * jnp.dot(
        total, mirror(taps).astype(F32), precision=lax.Precision.HIGHEST, preferred_element_type=F32
    )


def input_grads_body(member, band_ref, grad_ref, after_ref, keys_ref, values_ref, gated_ref, conv_ref, *refs):
    chan = grad_ref.shape[1]
    *term_refs, q_ref, k_ref, v_ref, filter_ref = refs
    total = term_refs[0][...]
    for ref in term_refs[1:]:
        total = total + ref[...]
    filter_ref[...] = total
    for tile in range(chan // LANES):
        columns = pl.ds(tile * LANES, LANES)
        mixed_grad = filtered(band_ref, grad_ref, after_ref, columns, member)
        k_ref[:, columns] = (mixed_grad * values_ref[:, columns].astype(F32)).astype(BF16)
        v_ref[:, columns] = (mixed_grad * keys_ref[:, columns].astype(F32)).astype(BF16)
        q_ref[:, columns] = (gated_ref[:, columns] * conv_ref[:, columns]).astype(BF16)


def shift(value, axis, by):
    devices = lax.axis_size(axis)
    return lax.ppermute(value, axis, [(i, i + by) for i in range(devices) if 0 <= i + by < devices])


def swap(value, mask):
    devices = lax.axis_size("tensor")
    return lax.ppermute(value, "tensor", [(i, i ^ mask) for i in range(devices)])


def over_dp(terms):
    devices = lax.axis_size("dp")
    if devices > 4:
        return [lax.psum(terms, "dp")]
    return [terms] + [
        lax.ppermute(terms, "dp", [(i, (i + by) % devices) for i in range(devices)]) for by in range(1, devices)
    ]


def on_device(queries, keys, values, doc_start, filters, out_weight, out_grad):
    rows, chan = queries.shape
    groups, taps = filters.shape
    member = chan // groups
    n = lax.axis_size("tensor")
    width = out_weight.shape[1] // n
    assert rows == taps == LANES and LANES % member == 0
    doc = doc_start.reshape(1, rows)
    tile, tile32, block = ((rows, chan), BF16), ((rows, chan), F32), ((rows, width), BF16)
    bands = pltpu.VMEM((groups * taps, 2 * taps), BF16)

    mixed = (keys.astype(F32) * values.astype(F32)).astype(BF16)
    before = shift(mixed, "dp", 1)
    hbm = pl.BlockSpec(memory_space=pltpu.HBM)
    fwd, bwd, gated_grad, conv_grad, leading, weight = pl.pallas_call(
        functools.partial(front_body, 2),
        out_shape=[bands, bands] + [jax.ShapeDtypeStruct(*s) for s in (tile32, tile, tile)] + [pltpu.VMEM(out_weight.shape, BF16)],
        in_specs=[hbm] * 5,
        out_specs=[VMEM] * 6,
        scratch_shapes=[
            pltpu.VMEM(doc.shape, jnp.int32), pltpu.VMEM((groups, taps), F32), pltpu.VMEM((groups, taps), F32),
            pltpu.VMEM(out_grad.shape, BF16), pltpu.VMEM(out_grad.shape[::-1], BF16), pltpu.VMEM(queries.shape, BF16),
            pltpu.SemaphoreType.DMA((max(1, chan // (2 * LANES)),)), pltpu.SemaphoreType.DMA((4,)),
        ],
        compiler_params=pltpu.CompilerParams(vmem_limit_bytes=16 * MIB),
        cost_estimate=cost(6.5),
        name="front",
    )(*(pltpu.with_memory_space_constraint(v, pltpu.HBM) for v in (doc, filters, out_grad, out_weight, queries)))
    fwd, bwd = held_in_vmem(fwd), held_in_vmem(bwd)

    if n == 8:
        some, rest = (3, 1), (2, 0)
        pair = ((2 * rows, width), BF16)
        weight, conv, gated, first = call(
            functools.partial(conv_body, member, some), (fwd, mixed, before, queries, weight),
            [tile32, tile, pair], "conv", 1.9, held=4,
        )
        first = swap(first, 1)
        weight, second = call(functools.partial(part_body, rest, True), (weight, gated), [pair], "part_rest", 0.8, held=0)
        second = swap(second, 1)
        weight, far, near_x = call(
            functools.partial(part_body, some, False), (weight, gated, first), [block, block], "sum_some", 0.8, held=0
        )
        far, near_x = swap(far, 6), swap(near_x, 2)
        weight, near_y, own = call(
            functools.partial(part_body, rest, False), (weight, gated, second), [block, block], "sum_rest", 0.8, held=0
        )
        near_y, leading, conv_grad = lax.optimization_barrier((near_y, leading, conv_grad))
        near_y = swap(near_y, 4)
        output = sum(v.astype(F32) for v in (own, near_x, near_y, far)).astype(BF16)
    else:
        weight, conv, gated = call(
            functools.partial(conv_body, member, ()), (fwd, mixed, before, queries, weight), [tile32, tile], "conv", 1.2, held=4
        )
        partial_out = jnp.dot(gated, out_weight, preferred_element_type=F32).astype(BF16)
        output = lax.psum_scatter(partial_out, "tensor", scatter_dimension=1, tiled=True)
    after = shift(leading, "dp", -1)
    scale = (rows * lax.axis_size("dp") * member) ** (-0.5)
    (terms,) = call(
        functools.partial(filter_grad_body, member, scale), (doc, conv_grad, mixed, before),
        [((groups, taps), F32)], "filter_grad", 1.7, scratch=[pltpu.VMEM((groups, SUBLANES, taps), F32)],
    )
    terms = over_dp(terms)
    q_grad, k_grad, v_grad, filter_grad = call(
        functools.partial(input_grads_body, member), (bwd, conv_grad, after, keys, values, gated_grad, conv, *terms),
        [tile, tile, tile, ((groups, taps), F32)], "input_grads", 2.0,
    )
    return (output, q_grad, k_grad, v_grad, filter_grad)


def solution(mesh):
    split = P("dp", "tensor")
    return jax.shard_map(
        on_device,
        mesh=mesh,
        in_specs=(split, split, split, P("dp"), P("tensor", None), P("tensor", None), P("dp", None)),
        out_specs=(split, split, split, split, P("tensor", None)),
        check_vma=False,
    )
```

```python
import functools

import jax
import jax.numpy as jnp
from jax import lax
from jax.experimental import pallas as pl
from jax.experimental.pallas import tpu as pltpu
from jax.sharding import PartitionSpec as P

F32, BF16 = jnp.float32, jnp.bfloat16
LANES = 128
SUBLANES = 8
NT = (((1,), (1,)), ((), ()))
VMEM = pl.BlockSpec(memory_space=pltpu.VMEM)
MIB = 1 << 20


def cost(us):
    return pl.CostEstimate(flops=int(us * 1.1e9), bytes_accessed=int(us * 3.6e6), transcendentals=0)


def call(body, operands, outs, name, us, scratch=(), held=None, hbm=0):
    shapes = [jax.ShapeDtypeStruct(*s) for s in outs]
    operands, aliases = list(operands), {}
    for k in range(hbm):
        operands[k] = pltpu.with_memory_space_constraint(operands[k], pltpu.HBM)
    if held is not None:
        operands[held] = held_in_vmem(operands[held])
        shapes = [pltpu.VMEM(operands[held].shape, operands[held].dtype)] + shapes
        aliases = {held: 0}
    return pl.pallas_call(
        body,
        out_shape=shapes,
        in_specs=[pl.BlockSpec(memory_space=pltpu.HBM)] * hbm + [VMEM] * (len(operands) - hbm),
        out_specs=[VMEM] * len(shapes),
        input_output_aliases=aliases,
        scratch_shapes=list(scratch),
        compiler_params=pltpu.CompilerParams(vmem_limit_bytes=16 * MIB),
        cost_estimate=cost(us),
        name=name,
    )(*operands)


def held_in_vmem(value):
    return pltpu.with_memory_space_constraint(value, pltpu.VMEM)


def apart(body):
    pl.when(lax.axis_index("dp") >= 0)(body)


def mirror(taps):
    i = lax.broadcasted_iota(jnp.int32, (taps, taps), 0)
    j = lax.broadcasted_iota(jnp.int32, (taps, taps), 1)
    return (i + j == taps) | ((i == 0) & (j == 0))


def doc_offsets(doc_ref, taps):
    first = lax.axis_index("dp") * taps
    lane = jnp.broadcast_to((doc_ref[...] - first).astype(F32), (taps, taps))
    return lane, lane.T


def grid_of(taps):
    return (
        lax.broadcasted_iota(jnp.int32, (taps, taps), 0).astype(F32),
        lax.broadcasted_iota(jnp.int32, (taps, taps), 1).astype(F32),
    )


def row_masks(doc_ref, taps):
    _, doc = doc_offsets(doc_ref, taps)
    t, s = grid_of(taps)
    return (s <= t) & (s >= doc), (s > t) & (s - taps >= doc)


def column_masks(doc_ref, taps):
    doc, _ = doc_offsets(doc_ref, taps)
    s, t = grid_of(taps)
    return (s <= t) & (s >= doc), (s > t) & (s >= doc[:, taps - 1 :])


def front_body(blocks, late, ahead, doc_hbm, filt_hbm, grad_hbm, weight_hbm, fwd_ref, bwd_ref, total_ref, late_ref,
               weight_ref, doc_ref, filt_ref, turned, grad_ref, came, arrived, landed):
    groups, taps = filt_ref.shape
    blocks, late = blocks(), late()
    count = len(blocks)
    share = -(-groups // count)
    small = [
        pltpu.make_async_copy(src, dst, came.at[k])
        for k, (src, dst) in enumerate(((doc_hbm, doc_ref), (filt_hbm, filt_ref)))
    ]
    grads = [
        pltpu.make_async_copy(grad_hbm.at[:, b], grad_ref.at[:, b], arrived.at[k]) for k, b in enumerate(blocks + late)
    ]
    weights = [
        pltpu.make_async_copy(weight_hbm.at[:, b], weight_ref.at[:, b], landed.at[k]) for k, b in enumerate(blocks)
    ]
    for copy in small + grads[:1] + weights[:1] + grads[1:] + weights[1:ahead]:
        copy.start()
    small[0].wait()
    here, before = [m.astype(BF16) for m in row_masks(doc_ref, taps)]
    here_t, after = [m.astype(BF16) for m in column_masks(doc_ref, taps)]
    small[1].wait()
    turned[...] = jnp.dot(filt_ref[...].astype(BF16), mirror(taps).astype(BF16), preferred_element_type=F32)

    def circulant(ref, g):
        line = jnp.broadcast_to(ref[pl.ds(g, 1), :], (taps, taps))
        return pltpu.roll(line, 0, 1, stride=1, stride_axis=0).astype(BF16)

    def bands(start, stop):
        for g in range(start, min(groups, stop)):
            rows = pl.ds(g * taps, taps)
            fwd = circulant(turned, g)
            fwd_ref[rows, :taps] = fwd * here
            fwd_ref[rows, taps:] = fwd * before
            bwd = circulant(filt_ref, g)
            bwd_ref[rows, :taps] = bwd * here_t
            bwd_ref[rows, taps:] = bwd * after

    for k, columns in enumerate(blocks):
        grads[k].wait()
        weights[k].wait()
        if k + ahead < count:
            weights[k + ahead].start()

        @apart
        def _():
            part = jnp.dot(weight_ref[:, columns], grad_ref[:, columns].T, preferred_element_type=F32)
            total_ref[...] = part if k == 0 else total_ref[...] + part
            bands(k * share, (k + 1) * share)

    for k, columns in enumerate(late):
        grads[count + k].wait()
        width = columns.size
        late_ref[pl.ds(k * width, width), :] = grad_ref[:, columns].T


def gated_grad_body(late, doc_ref, weight_ref, total_ref, late_ref, queries_ref, held_ref, gated_ref, conv_ref, lead_ref):
    del held_ref
    taps = doc_ref.shape[1]
    total = total_ref[...]
    for k, columns in enumerate(late()):
        width = columns.size
        total = total + jnp.dot(weight_ref[:, columns], late_ref[pl.ds(k * width, width), :], preferred_element_type=F32)
    total = total.T
    gated_ref[...] = total
    conv_grad = (total * queries_ref[...].astype(F32)).astype(BF16)
    conv_ref[...] = conv_grad
    _, doc = doc_offsets(doc_ref, taps)
    lead_ref[...] = jnp.where(doc[:, :1] < 0, conv_grad, jnp.zeros_like(conv_grad))


def filtered(band_ref, near_ref, far_ref, columns, member):
    taps = near_ref.shape[0]
    groups = LANES // member
    both = jnp.concatenate([near_ref[:, columns], far_ref[:, columns]], axis=0)
    bands = pl.ds(columns.start // LANES * groups * taps, groups * taps)
    every = jnp.dot(band_ref[bands, :], both, preferred_element_type=F32)
    owner = lax.div(lax.broadcasted_iota(jnp.int32, (taps, LANES), 1), member)
    total = every[:taps]
    for g in range(1, groups):
        total = jnp.where(owner == g, every[g * taps : (g + 1) * taps], total)
    return total


def block_columns(offset, sibling, width):
    me = lax.axis_index("tensor")
    chip, core = lax.div(me, 2), lax.rem(me, 2)
    owner = 2 * jnp.bitwise_xor(chip, offset) + (1 - core if sibling else core)
    return pl.ds(pl.multiple_of(owner * width, width), width)


def conv_body(member, offsets, late, weight_hbm, band_ref, mixed_ref, before_ref, queries_ref, weight_ref, held_ref, conv_ref, gated_ref, *refs):
    *part_refs, landed = refs
    copies = [pltpu.make_async_copy(weight_hbm.at[:, b], held_ref.at[:, b], landed.at[k]) for k, b in enumerate(late())]
    for copy in copies:
        copy.start()

    @apart
    def _():
        for tile in range(mixed_ref.shape[1] // LANES):
            columns = pl.ds(tile * LANES, LANES)
            conv = filtered(band_ref, mixed_ref, before_ref, columns, member)
            conv_ref[:, columns] = conv
            gated_ref[:, columns] = (queries_ref[:, columns].astype(F32) * conv).astype(BF16)
        part_body(offsets, True, held_ref, gated_ref, *part_refs)

    for copy in copies:
        copy.wait()


def part_body(offsets, sibling, weight_ref, gated_ref, *refs):
    rows = gated_ref.shape[0]
    for k, offset in enumerate(offsets):
        width = refs[-1].shape[1]
        stacked = pl.ds(k * rows, rows)
        columns = block_columns(offset, sibling, width)
        part = jnp.dot(gated_ref[...], weight_ref[:, columns], preferred_element_type=F32)
        if sibling:
            refs[-1][stacked, :] = part.astype(BF16)
        else:
            summed = part.astype(BF16).astype(F32) + refs[0][stacked, :].astype(F32)
            refs[k - len(offsets)][...] = summed.astype(BF16)


def filter_grad_body(member, scale, doc_ref, grad_ref, mixed_ref, before_ref, out_ref, sums):
    taps, chan = grad_ref.shape
    groups = LANES // member
    here, before = [m.astype(F32) for m in row_masks(doc_ref, taps)]
    owner = lax.div(lax.broadcasted_iota(jnp.int32, (taps, LANES), 1), member)

    for tile in range(chan // LANES):
        columns = pl.ds(tile * LANES, LANES)
        both = jnp.concatenate([mixed_ref[:, columns], before_ref[:, columns]], axis=0)
        grad = grad_ref[:, columns]
        apart = jnp.concatenate([grad * (owner == g).astype(BF16) for g in range(groups)], axis=0)
        every = lax.dot_general(apart, both, NT, preferred_element_type=F32)
        for g in range(groups):
            one = every[g * taps : (g + 1) * taps]
            one = one[:, :taps] * here + one[:, taps:] * before
            total = one[:SUBLANES]
            for b in range(SUBLANES, taps, SUBLANES):
                total = total + pltpu.roll(one[b : b + SUBLANES], taps - b, 1)
            sums[tile * groups + g] = total

    total = sums[:, 0, :]
    for i in range(1, SUBLANES):
        total = total + pltpu.roll(sums[:, i, :], taps - i, 1)
    out_ref[...] = scale * jnp.dot(
        total, mirror(taps).astype(F32), precision=lax.Precision.HIGHEST, preferred_element_type=F32
    )


def input_grads_body(member, band_ref, grad_ref, after_ref, keys_ref, values_ref, gated_ref, conv_ref, *refs):
    chan = grad_ref.shape[1]
    q_ref, k_ref, v_ref = refs
    for tile in range(chan // LANES):
        columns = pl.ds(tile * LANES, LANES)
        mixed_grad = filtered(band_ref, grad_ref, after_ref, columns, member)
        k_ref[:, columns] = (mixed_grad * values_ref[:, columns].astype(F32)).astype(BF16)
        v_ref[:, columns] = (mixed_grad * keys_ref[:, columns].astype(F32)).astype(BF16)
        q_ref[:, columns] = (gated_ref[:, columns] * conv_ref[:, columns]).astype(BF16)


def finish_body(count, *refs):
    *parts, out_ref, filter_ref = refs
    out_ref[...] = sum(ref[...].astype(F32) for ref in parts[count:]).astype(BF16)
    filter_ref[...] = sum(ref[...] for ref in parts[:count])


def shift(value, axis, by):
    devices = lax.axis_size(axis)
    return lax.ppermute(value, axis, [(i, i + by) for i in range(devices) if 0 <= i + by < devices])


def swap(value, mask):
    devices = lax.axis_size("tensor")
    return lax.ppermute(value, "tensor", [(i, i ^ mask) for i in range(devices)])


def turn(value, by):
    devices = lax.axis_size("dp")
    return lax.ppermute(value, "dp", [(i, (i + by) % devices) for i in range(devices)])


def on_device(queries, keys, values, doc_start, filters, out_weight, out_grad):
    rows, chan = queries.shape
    groups, taps = filters.shape
    member = chan // groups
    n = lax.axis_size("tensor")
    width = out_weight.shape[1] // n
    assert rows == taps == LANES and LANES % member == 0
    doc = doc_start.reshape(1, rows)
    tile, tile32, block = ((rows, chan), BF16), ((rows, chan), F32), ((rows, width), BF16)
    bands = pltpu.VMEM((groups * taps, 2 * taps), BF16)

    mixed = (keys.astype(F32) * values.astype(F32)).astype(BF16)
    before = shift(mixed, "dp", 1)
    staged = n == 8 and lax.axis_size("dp") == 4
    some, rest = (3, 1), (2, 0)
    if staged:
        at = lambda pairs: [block_columns(offset, sibling, width) for sibling, offsets in pairs for offset in offsets]
        blocks = functools.partial(at, ((True, some), (True, rest), (False, some)))
        late = functools.partial(at, ((False, rest),))
        early_count, late_count = 6, 2
    else:
        early_count, late_count = 8, 0
        step = out_weight.shape[1] // early_count
        blocks, late = lambda: [pl.ds(k * step, step) for k in range(early_count)], lambda: []
    late_rows = max(late_count * width, LANES)
    fwd, bwd, total, late_grad, weight = pl.pallas_call(
        functools.partial(front_body, blocks, late, 6),
        out_shape=[bands, bands] + [jax.ShapeDtypeStruct(*s) for s in (((chan, rows), F32), ((late_rows, rows), BF16))]
        + [pltpu.VMEM(out_weight.shape, BF16)],
        in_specs=[pl.BlockSpec(memory_space=pltpu.HBM)] * 4,
        out_specs=[VMEM] * 5,
        scratch_shapes=[
            pltpu.VMEM(doc.shape, jnp.int32), pltpu.VMEM((groups, taps), F32), pltpu.VMEM((groups, taps), F32),
            pltpu.VMEM(out_grad.shape, BF16), pltpu.SemaphoreType.DMA((2,)),
            pltpu.SemaphoreType.DMA((early_count + late_count,)), pltpu.SemaphoreType.DMA((early_count,)),
        ],
        compiler_params=pltpu.CompilerParams(vmem_limit_bytes=16 * MIB),
        cost_estimate=cost(6.0),
        name="front",
    )(*(pltpu.with_memory_space_constraint(v, pltpu.HBM) for v in (doc, filters, out_grad, out_weight)))
    fwd, bwd = held_in_vmem(fwd), held_in_vmem(bwd)

    landed = [pltpu.SemaphoreType.DMA((max(1, late_count),))]
    finish_gated = functools.partial(gated_grad_body, late)
    if staged:
        pair = ((2 * rows, width), BF16)
        weight, conv, gated, first = call(
            functools.partial(conv_body, member, some, late), (out_weight, fwd, mixed, before, queries, weight),
            [tile32, tile, pair], "conv", 1.9, held=5, hbm=1, scratch=landed,
        )
        first = swap(first, 1)
        weight, second = call(functools.partial(part_body, rest, True), (weight, gated), [pair], "part_rest", 0.8, held=0)
        second = swap(second, 1)
        weight, gated_grad, conv_grad, leading = call(
            finish_gated, (doc, weight, total, late_grad, queries), [tile32, tile, tile], "gated_grad", 1.5, held=1
        )
        weight, far, near_x = call(
            functools.partial(part_body, some, False), (weight, gated, first), [block, block], "sum_some", 0.8, held=0
        )
        far, near_x = swap(far, 6), swap(near_x, 2)
        weight, near_y, own = call(
            functools.partial(part_body, rest, False), (weight, gated, second), [block, block], "sum_rest", 0.8, held=0
        )
        near_y = swap(near_y, 4)
    else:
        weight, conv, gated = call(
            functools.partial(conv_body, member, (), late), (out_weight, fwd, mixed, before, queries, weight),
            [tile32, tile], "conv", 1.2, held=5, hbm=1, scratch=landed,
        )
        weight, gated_grad, conv_grad, leading = call(
            finish_gated, (doc, weight, total, late_grad, queries), [tile32, tile, tile], "gated_grad", 1.5, held=1
        )
        partial_out = jnp.dot(gated, out_weight, preferred_element_type=F32).astype(BF16)
        output = lax.psum_scatter(partial_out, "tensor", scatter_dimension=1, tiled=True)
    after = shift(leading, "dp", -1)
    scale = (rows * lax.axis_size("dp") * member) ** (-0.5)
    (terms,) = call(
        functools.partial(filter_grad_body, member, scale), (doc, conv_grad, mixed, before),
        [((groups, taps), F32)], "filter_grad", 1.7, scratch=[pltpu.VMEM((groups, SUBLANES, taps), F32)],
    )
    if staged:
        terms = terms + lax.ppermute(terms, "dp", [(i, i ^ 1) for i in range(4)])
        terms = (terms, turn(terms, 2))
    else:
        terms = (lax.psum(terms, "dp"),)
    q_grad, k_grad, v_grad = call(
        functools.partial(input_grads_body, member), (bwd, conv_grad, after, keys, values, gated_grad, conv),
        [tile, tile, tile], "input_grads", 2.0,
    )
    if staged:
        output, filter_grad = call(
            functools.partial(finish_body, len(terms)), (*terms, own, near_x, near_y, far),
            [block, ((groups, taps), F32)], "finish", 0.9,
        )
    else:
        filter_grad = sum(terms)
    return (output, q_grad, k_grad, v_grad, filter_grad)


def solution(mesh):
    split = P("dp", "tensor")
    return jax.shard_map(
        on_device,
        mesh=mesh,
        in_specs=(split, split, split, P("dp"), P("tensor", None), P("tensor", None), P("dp", None)),
        out_specs=(split, split, split, split, P("tensor", None)),
        check_vma=False,
    )
```

```python
import functools

import jax
import jax.numpy as jnp
from jax import lax
from jax.experimental import pallas as pl
from jax.experimental.pallas import tpu as pltpu
from jax.sharding import PartitionSpec as P

F32, BF16 = jnp.float32, jnp.bfloat16
LANES = 128
SUBLANES = 8
NT = (((1,), (1,)), ((), ()))
VMEM = pl.BlockSpec(memory_space=pltpu.VMEM)
MIB = 1 << 20


def cost(us):
    return pl.CostEstimate(flops=int(us * 1.1e9), bytes_accessed=int(us * 3.6e6), transcendentals=0)


def call(body, operands, outs, name, us, scratch=(), held=None, hbm=0):
    shapes = [jax.ShapeDtypeStruct(*s) for s in outs]
    operands, aliases = list(operands), {}
    for k in range(hbm):
        operands[k] = pltpu.with_memory_space_constraint(operands[k], pltpu.HBM)
    if held is not None:
        operands[held] = held_in_vmem(operands[held])
        shapes = [pltpu.VMEM(operands[held].shape, operands[held].dtype)] + shapes
        aliases = {held: 0}
    return pl.pallas_call(
        body,
        out_shape=shapes,
        in_specs=[pl.BlockSpec(memory_space=pltpu.HBM)] * hbm + [VMEM] * (len(operands) - hbm),
        out_specs=[VMEM] * len(shapes),
        input_output_aliases=aliases,
        scratch_shapes=list(scratch),
        compiler_params=pltpu.CompilerParams(vmem_limit_bytes=16 * MIB),
        cost_estimate=cost(us),
        name=name,
    )(*operands)


def held_in_vmem(value):
    return pltpu.with_memory_space_constraint(value, pltpu.VMEM)


def apart(body):
    pl.when(lax.axis_index("dp") >= 0)(body)


def mirror(taps):
    i = lax.broadcasted_iota(jnp.int32, (taps, taps), 0)
    j = lax.broadcasted_iota(jnp.int32, (taps, taps), 1)
    return (i + j == taps) | ((i == 0) & (j == 0))


def doc_offsets(doc_ref, taps):
    first = lax.axis_index("dp") * taps
    lane = jnp.broadcast_to((doc_ref[...] - first).astype(F32), (taps, taps))
    return lane, lane.T


def grid_of(taps):
    return (
        lax.broadcasted_iota(jnp.int32, (taps, taps), 0).astype(F32),
        lax.broadcasted_iota(jnp.int32, (taps, taps), 1).astype(F32),
    )


def row_masks(doc_ref, taps):
    _, doc = doc_offsets(doc_ref, taps)
    t, s = grid_of(taps)
    return (s <= t) & (s >= doc), (s > t) & (s - taps >= doc)


def column_masks(doc_ref, taps):
    doc, _ = doc_offsets(doc_ref, taps)
    s, t = grid_of(taps)
    return (s <= t) & (s >= doc), (s > t) & (s >= doc[:, taps - 1 :])


def front_body(blocks, late, ahead, doc_hbm, filt_hbm, grad_hbm, weight_hbm, fwd_ref, bwd_ref, total_ref, late_ref,
               weight_ref, doc_ref, filt_ref, turned, grad_ref, came, arrived, landed):
    groups, taps = filt_ref.shape
    blocks, late = blocks(), late()
    count = len(blocks)
    share = -(-groups // max(1, count - 1))
    small = [
        pltpu.make_async_copy(src, dst, came.at[k])
        for k, (src, dst) in enumerate(((doc_hbm, doc_ref), (filt_hbm, filt_ref)))
    ]
    grads = [
        pltpu.make_async_copy(grad_hbm.at[:, b], grad_ref.at[:, b], arrived.at[k]) for k, b in enumerate(blocks + late)
    ]
    weights = [
        pltpu.make_async_copy(weight_hbm.at[:, b], weight_ref.at[:, b], landed.at[k]) for k, b in enumerate(blocks)
    ]
    for copy in small + grads[:1] + weights[:1] + grads[1:] + weights[1:ahead]:
        copy.start()
    small[0].wait()
    here, before = [m.astype(BF16) for m in row_masks(doc_ref, taps)]
    here_t, after = [m.astype(BF16) for m in column_masks(doc_ref, taps)]
    small[1].wait()
    turned[...] = jnp.dot(filt_ref[...].astype(BF16), mirror(taps).astype(BF16), preferred_element_type=F32)

    def circulant(ref, g):
        line = jnp.broadcast_to(ref[pl.ds(g, 1), :], (taps, taps))
        return pltpu.roll(line, 0, 1, stride=1, stride_axis=0).astype(BF16)

    def bands(start, stop):
        for g in range(start, min(groups, stop)):
            rows = pl.ds(g * taps, taps)
            fwd = circulant(turned, g)
            fwd_ref[rows, :taps] = fwd * here
            fwd_ref[rows, taps:] = fwd * before
            bwd = circulant(filt_ref, g)
            bwd_ref[rows, :taps] = bwd * here_t
            bwd_ref[rows, taps:] = bwd * after

    for k, columns in enumerate(blocks):
        grads[k].wait()
        weights[k].wait()
        if k + ahead < count:
            weights[k + ahead].start()

        @apart
        def _():
            part = jnp.dot(weight_ref[:, columns], grad_ref[:, columns].T, preferred_element_type=F32)
            total_ref[...] = part if k == 0 else total_ref[...] + part
            bands(k * share, (k + 1) * share)

    for k, columns in enumerate(late):
        grads[count + k].wait()
        width = columns.size
        late_ref[pl.ds(k * width, width), :] = grad_ref[:, columns].T


def gated_grad_body(late, doc_ref, weight_ref, total_ref, late_ref, queries_ref, held_ref, gated_ref, conv_ref, lead_ref):
    del held_ref
    taps = doc_ref.shape[1]
    total = total_ref[...]
    for k, columns in enumerate(late()):
        width = columns.size
        total = total + jnp.dot(weight_ref[:, columns], late_ref[pl.ds(k * width, width), :], preferred_element_type=F32)
    total = total.T
    gated_ref[...] = total
    conv_grad = (total * queries_ref[...].astype(F32)).astype(BF16)
    conv_ref[...] = conv_grad
    _, doc = doc_offsets(doc_ref, taps)
    lead_ref[...] = jnp.where(doc[:, :1] < 0, conv_grad, jnp.zeros_like(conv_grad))


def filtered(band_ref, near_ref, far_ref, columns, member):
    taps = near_ref.shape[0]
    groups = LANES // member
    both = jnp.concatenate([near_ref[:, columns], far_ref[:, columns]], axis=0)
    bands = pl.ds(columns.start // LANES * groups * taps, groups * taps)
    every = jnp.dot(band_ref[bands, :], both, preferred_element_type=F32)
    owner = lax.div(lax.broadcasted_iota(jnp.int32, (taps, LANES), 1), member)
    total = every[:taps]
    for g in range(1, groups):
        total = jnp.where(owner == g, every[g * taps : (g + 1) * taps], total)
    return total


def block_columns(offset, sibling, width):
    me = lax.axis_index("tensor")
    chip, core = lax.div(me, 2), lax.rem(me, 2)
    owner = 2 * jnp.bitwise_xor(chip, offset) + (1 - core if sibling else core)
    return pl.ds(pl.multiple_of(owner * width, width), width)


def conv_body(member, offsets, late, weight_hbm, band_ref, mixed_ref, before_ref, queries_ref, weight_ref, held_ref, conv_ref, gated_ref, *refs):
    *part_refs, landed = refs
    copies = [pltpu.make_async_copy(weight_hbm.at[:, b], held_ref.at[:, b], landed.at[k]) for k, b in enumerate(late())]
    for copy in copies:
        copy.start()

    @apart
    def _():
        for tile in range(mixed_ref.shape[1] // LANES):
            columns = pl.ds(tile * LANES, LANES)
            conv = filtered(band_ref, mixed_ref, before_ref, columns, member)
            conv_ref[:, columns] = conv
            gated_ref[:, columns] = (queries_ref[:, columns].astype(F32) * conv).astype(BF16)
        part_body(offsets, True, held_ref, gated_ref, *part_refs)

    for copy in copies:
        copy.wait()


def part_body(offsets, sibling, weight_ref, gated_ref, *refs):
    rows = gated_ref.shape[0]
    for k, offset in enumerate(offsets):
        width = refs[-1].shape[1]
        stacked = pl.ds(k * rows, rows)
        columns = block_columns(offset, sibling, width)
        part = jnp.dot(gated_ref[...], weight_ref[:, columns], preferred_element_type=F32)
        if sibling:
            refs[-1][stacked, :] = part.astype(BF16)
        else:
            summed = part.astype(BF16).astype(F32) + refs[0][stacked, :].astype(F32)
            refs[k - len(offsets)][...] = summed.astype(BF16)


def filter_grad_body(member, scale, doc_ref, grad_ref, mixed_ref, before_ref, out_ref, sums):
    taps, chan = grad_ref.shape
    groups = LANES // member
    here, before = [m.astype(F32) for m in row_masks(doc_ref, taps)]
    owner = lax.div(lax.broadcasted_iota(jnp.int32, (taps, LANES), 1), member)

    for tile in range(chan // LANES):
        columns = pl.ds(tile * LANES, LANES)
        both = jnp.concatenate([mixed_ref[:, columns], before_ref[:, columns]], axis=0)
        grad = grad_ref[:, columns]
        apart = jnp.concatenate([grad * (owner == g).astype(BF16) for g in range(groups)], axis=0)
        every = lax.dot_general(apart, both, NT, preferred_element_type=F32)
        for g in range(groups):
            one = every[g * taps : (g + 1) * taps]
            one = one[:, :taps] * here + one[:, taps:] * before
            total = one[:SUBLANES]
            for b in range(SUBLANES, taps, SUBLANES):
                total = total + pltpu.roll(one[b : b + SUBLANES], taps - b, 1)
            sums[tile * groups + g] = total

    total = sums[:, 0, :]
    for i in range(1, SUBLANES):
        total = total + pltpu.roll(sums[:, i, :], taps - i, 1)
    out_ref[...] = scale * jnp.dot(
        total, mirror(taps).astype(F32), precision=lax.Precision.HIGHEST, preferred_element_type=F32
    )


def input_grads_body(member, band_ref, grad_ref, after_ref, keys_ref, values_ref, gated_ref, conv_ref, *refs):
    chan = grad_ref.shape[1]
    q_ref, k_ref, v_ref = refs
    for tile in range(chan // LANES):
        columns = pl.ds(tile * LANES, LANES)
        mixed_grad = filtered(band_ref, grad_ref, after_ref, columns, member)
        k_ref[:, columns] = (mixed_grad * values_ref[:, columns].astype(F32)).astype(BF16)
        v_ref[:, columns] = (mixed_grad * keys_ref[:, columns].astype(F32)).astype(BF16)
        q_ref[:, columns] = (gated_ref[:, columns] * conv_ref[:, columns]).astype(BF16)


def finish_body(count, *refs):
    *parts, out_ref, filter_ref = refs
    out_ref[...] = sum(ref[...].astype(F32) for ref in parts[count:]).astype(BF16)
    filter_ref[...] = sum(ref[...] for ref in parts[:count])


def shift(value, axis, by):
    devices = lax.axis_size(axis)
    return lax.ppermute(value, axis, [(i, i + by) for i in range(devices) if 0 <= i + by < devices])


def swap(value, mask):
    devices = lax.axis_size("tensor")
    return lax.ppermute(value, "tensor", [(i, i ^ mask) for i in range(devices)])


def turn(value, by):
    devices = lax.axis_size("dp")
    return lax.ppermute(value, "dp", [(i, (i + by) % devices) for i in range(devices)])


def on_device(queries, keys, values, doc_start, filters, out_weight, out_grad):
    rows, chan = queries.shape
    groups, taps = filters.shape
    member = chan // groups
    n = lax.axis_size("tensor")
    width = out_weight.shape[1] // n
    assert rows == taps == LANES and LANES % member == 0
    doc = doc_start.reshape(1, rows)
    tile, tile32, block = ((rows, chan), BF16), ((rows, chan), F32), ((rows, width), BF16)
    bands = pltpu.VMEM((groups * taps, 2 * taps), BF16)

    mixed = (keys.astype(F32) * values.astype(F32)).astype(BF16)
    before = shift(mixed, "dp", 1)
    staged = n == 8 and lax.axis_size("dp") == 4
    some, rest = (3, 1), (2, 0)
    if staged:
        at = lambda pairs: [block_columns(offset, sibling, width) for sibling, offsets in pairs for offset in offsets]
        blocks = functools.partial(at, ((True, some), (True, rest), (False, (3, 1, 2))))
        late = functools.partial(at, ((False, (0,)),))
        early_count, late_count = 7, 1
    else:
        early_count, late_count = 8, 0
        step = out_weight.shape[1] // early_count
        blocks, late = lambda: [pl.ds(k * step, step) for k in range(early_count)], lambda: []
    late_rows = max(late_count * width, LANES)
    fwd, bwd, total, late_grad, weight = pl.pallas_call(
        functools.partial(front_body, blocks, late, 7),
        out_shape=[bands, bands] + [jax.ShapeDtypeStruct(*s) for s in (((chan, rows), F32), ((late_rows, rows), BF16))]
        + [pltpu.VMEM(out_weight.shape, BF16)],
        in_specs=[pl.BlockSpec(memory_space=pltpu.HBM)] * 4,
        out_specs=[VMEM] * 5,
        scratch_shapes=[
            pltpu.VMEM(doc.shape, jnp.int32), pltpu.VMEM((groups, taps), F32), pltpu.VMEM((groups, taps), F32),
            pltpu.VMEM(out_grad.shape, BF16), pltpu.SemaphoreType.DMA((2,)),
            pltpu.SemaphoreType.DMA((early_count + late_count,)), pltpu.SemaphoreType.DMA((early_count,)),
        ],
        compiler_params=pltpu.CompilerParams(vmem_limit_bytes=16 * MIB),
        cost_estimate=cost(6.0),
        name="front",
    )(*(pltpu.with_memory_space_constraint(v, pltpu.HBM) for v in (doc, filters, out_grad, out_weight)))
    fwd, bwd = held_in_vmem(fwd), held_in_vmem(bwd)

    landed = [pltpu.SemaphoreType.DMA((max(1, late_count),))]
    finish_gated = functools.partial(gated_grad_body, late)
    if staged:
        stack = ((len(some + rest) * rows, width), BF16)
        weight, conv, gated, came = call(
            functools.partial(conv_body, member, some + rest, late), (out_weight, fwd, mixed, before, queries, weight),
            [tile32, tile, stack], "conv", 2.6, held=5, hbm=1, scratch=landed,
        )
        came = swap(came, 1)
        weight, gated_grad, conv_grad, leading = call(
            finish_gated, (doc, weight, total, late_grad, queries), [tile32, tile, tile], "gated_grad", 1.5, held=1
        )
        weight, far, near_x, near_y, own = call(
            functools.partial(part_body, some + rest, False), (weight, gated, came), [block] * 4, "sums", 1.4, held=0
        )
        far, near_x, near_y = swap(far, 6), swap(near_x, 2), swap(near_y, 4)
    else:
        weight, conv, gated = call(
            functools.partial(conv_body, member, (), late), (out_weight, fwd, mixed, before, queries, weight),
            [tile32, tile], "conv", 1.2, held=5, hbm=1, scratch=landed,
        )
        weight, gated_grad, conv_grad, leading = call(
            finish_gated, (doc, weight, total, late_grad, queries), [tile32, tile, tile], "gated_grad", 1.5, held=1
        )
        partial_out = jnp.dot(gated, out_weight, preferred_element_type=F32).astype(BF16)
        output = lax.psum_scatter(partial_out, "tensor", scatter_dimension=1, tiled=True)
    after = shift(leading, "dp", -1)
    scale = (rows * lax.axis_size("dp") * member) ** (-0.5)
    (terms,) = call(
        functools.partial(filter_grad_body, member, scale), (doc, conv_grad, mixed, before),
        [((groups, taps), F32)], "filter_grad", 1.7, scratch=[pltpu.VMEM((groups, SUBLANES, taps), F32)],
    )
    if staged:
        terms = terms + lax.ppermute(terms, "dp", [(i, i ^ 1) for i in range(4)])
        terms = (terms, turn(terms, 2))
    else:
        terms = (lax.psum(terms, "dp"),)
    q_grad, k_grad, v_grad = call(
        functools.partial(input_grads_body, member), (bwd, conv_grad, after, keys, values, gated_grad, conv),
        [tile, tile, tile], "input_grads", 2.0,
    )
    if staged:
        output, filter_grad = call(
            functools.partial(finish_body, len(terms)), (*terms, own, near_x, near_y, far),
            [block, ((groups, taps), F32)], "finish", 0.9,
        )
    else:
        filter_grad = sum(terms)
    return (output, q_grad, k_grad, v_grad, filter_grad)


def solution(mesh):
    split = P("dp", "tensor")
    return jax.shard_map(
        on_device,
        mesh=mesh,
        in_specs=(split, split, split, P("dp"), P("tensor", None), P("tensor", None), P("dp", None)),
        out_specs=(split, split, split, split, P("tensor", None)),
        check_vma=False,
    )
```

```python
import functools

import jax
import jax.numpy as jnp
from jax import lax
from jax.experimental import pallas as pl
from jax.experimental.pallas import tpu as pltpu
from jax.sharding import PartitionSpec as P

F32, BF16 = jnp.float32, jnp.bfloat16
LANES = 128
SUBLANES = 8
NT = (((1,), (1,)), ((), ()))
VMEM = pl.BlockSpec(memory_space=pltpu.VMEM)
MIB = 1 << 20


def cost(us):
    return pl.CostEstimate(flops=int(us * 1.1e9), bytes_accessed=int(us * 3.6e6), transcendentals=0)


def call(body, operands, outs, name, us, scratch=(), held=None, hbm=0):
    shapes = [jax.ShapeDtypeStruct(*s) for s in outs]
    operands, aliases = list(operands), {}
    for k in range(hbm):
        operands[k] = pltpu.with_memory_space_constraint(operands[k], pltpu.HBM)
    if held is not None:
        operands[held] = held_in_vmem(operands[held])
        shapes = [pltpu.VMEM(operands[held].shape, operands[held].dtype)] + shapes
        aliases = {held: 0}
    return pl.pallas_call(
        body,
        out_shape=shapes,
        in_specs=[pl.BlockSpec(memory_space=pltpu.HBM)] * hbm + [VMEM] * (len(operands) - hbm),
        out_specs=[VMEM] * len(shapes),
        input_output_aliases=aliases,
        scratch_shapes=list(scratch),
        compiler_params=pltpu.CompilerParams(vmem_limit_bytes=16 * MIB),
        cost_estimate=cost(us),
        name=name,
    )(*operands)


def held_in_vmem(value):
    return pltpu.with_memory_space_constraint(value, pltpu.VMEM)


def apart(body):
    pl.when(lax.axis_index("dp") >= 0)(body)


def mirror(taps):
    i = lax.broadcasted_iota(jnp.int32, (taps, taps), 0)
    j = lax.broadcasted_iota(jnp.int32, (taps, taps), 1)
    return (i + j == taps) | ((i == 0) & (j == 0))


def doc_offsets(doc_ref, taps):
    first = lax.axis_index("dp") * taps
    lane = jnp.broadcast_to((doc_ref[...] - first).astype(F32), (taps, taps))
    return lane, lane.T


def grid_of(taps):
    return (
        lax.broadcasted_iota(jnp.int32, (taps, taps), 0).astype(F32),
        lax.broadcasted_iota(jnp.int32, (taps, taps), 1).astype(F32),
    )


def row_masks(doc_ref, taps):
    _, doc = doc_offsets(doc_ref, taps)
    t, s = grid_of(taps)
    return (s <= t) & (s >= doc), (s > t) & (s - taps >= doc)


def column_masks(doc_ref, taps):
    doc, _ = doc_offsets(doc_ref, taps)
    s, t = grid_of(taps)
    return (s <= t) & (s >= doc), (s > t) & (s >= doc[:, taps - 1 :])


def front_body(blocks, late, ahead, doc_hbm, filt_hbm, grad_hbm, weight_hbm, fwd_ref, bwd_ref, total_ref, late_ref,
               weight_ref, doc_ref, filt_ref, turned, grad_ref, came, arrived, landed):
    groups, taps = filt_ref.shape
    blocks, late = blocks(), late()
    count = len(blocks)
    share = -(-groups // max(1, count - 1))
    small = [
        pltpu.make_async_copy(src, dst, came.at[k])
        for k, (src, dst) in enumerate(((doc_hbm, doc_ref), (filt_hbm, filt_ref)))
    ]
    grads = [
        pltpu.make_async_copy(grad_hbm.at[:, b], grad_ref.at[:, b], arrived.at[k]) for k, b in enumerate(blocks + late)
    ]
    weights = [
        pltpu.make_async_copy(weight_hbm.at[:, b], weight_ref.at[:, b], landed.at[k]) for k, b in enumerate(blocks)
    ]
    for copy in small + grads[:1] + weights[:1] + grads[1:] + weights[1:ahead]:
        copy.start()
    small[0].wait()
    here, before = [m.astype(BF16) for m in row_masks(doc_ref, taps)]
    here_t, after = [m.astype(BF16) for m in column_masks(doc_ref, taps)]
    small[1].wait()
    turned[...] = jnp.dot(filt_ref[...].astype(BF16), mirror(taps).astype(BF16), preferred_element_type=F32)

    def circulant(ref, g):
        line = jnp.broadcast_to(ref[pl.ds(g, 1), :], (taps, taps))
        return pltpu.roll(line, 0, 1, stride=1, stride_axis=0).astype(BF16)

    def bands(start, stop):
        for g in range(start, min(groups, stop)):
            rows = pl.ds(g * taps, taps)
            fwd = circulant(turned, g)
            fwd_ref[rows, :taps] = fwd * here
            fwd_ref[rows, taps:] = fwd * before
            bwd = circulant(filt_ref, g)
            bwd_ref[rows, :taps] = bwd * here_t
            bwd_ref[rows, taps:] = bwd * after

    for k, columns in enumerate(blocks):
        grads[k].wait()
        weights[k].wait()
        if k + ahead < count:
            weights[k + ahead].start()

        @apart
        def _():
            part = jnp.dot(weight_ref[:, columns], grad_ref[:, columns].T, preferred_element_type=F32)
            total_ref[...] = part if k == 0 else total_ref[...] + part
            bands(k * share, (k + 1) * share)

    for k, columns in enumerate(late):
        grads[count + k].wait()
        width = columns.size
        late_ref[pl.ds(k * width, width), :] = grad_ref[:, columns].T


def gated_grad_body(late, doc_ref, weight_ref, total_ref, late_ref, queries_ref, held_ref, gated_ref, conv_ref, lead_ref):
    del held_ref
    taps = doc_ref.shape[1]
    total = total_ref[...]
    for k, columns in enumerate(late()):
        width = columns.size
        total = total + jnp.dot(weight_ref[:, columns], late_ref[pl.ds(k * width, width), :], preferred_element_type=F32)
    total = total.T
    gated_ref[...] = total
    conv_grad = (total * queries_ref[...].astype(F32)).astype(BF16)
    conv_ref[...] = conv_grad
    _, doc = doc_offsets(doc_ref, taps)
    lead_ref[...] = jnp.where(doc[:, :1] < 0, conv_grad, jnp.zeros_like(conv_grad))


def filtered(band_ref, near_ref, far_ref, columns, member):
    taps = near_ref.shape[0]
    groups = LANES // member
    both = jnp.concatenate([near_ref[:, columns], far_ref[:, columns]], axis=0)
    bands = pl.ds(columns.start // LANES * groups * taps, groups * taps)
    every = jnp.dot(band_ref[bands, :], both, preferred_element_type=F32)
    owner = lax.div(lax.broadcasted_iota(jnp.int32, (taps, LANES), 1), member)
    total = every[:taps]
    for g in range(1, groups):
        total = jnp.where(owner == g, every[g * taps : (g + 1) * taps], total)
    return total


def block_columns(offset, sibling, width):
    me = lax.axis_index("tensor")
    chip, core = lax.div(me, 2), lax.rem(me, 2)
    owner = 2 * jnp.bitwise_xor(chip, offset) + (1 - core if sibling else core)
    return pl.ds(pl.multiple_of(owner * width, width), width)


def conv_body(member, offsets, late, weight_hbm, band_ref, mixed_ref, before_ref, queries_ref, weight_ref, held_ref, conv_ref, gated_ref, *refs):
    *part_refs, landed = refs
    copies = [pltpu.make_async_copy(weight_hbm.at[:, b], held_ref.at[:, b], landed.at[k]) for k, b in enumerate(late())]
    for copy in copies:
        copy.start()

    @apart
    def _():
        for tile in range(mixed_ref.shape[1] // LANES):
            columns = pl.ds(tile * LANES, LANES)
            conv = filtered(band_ref, mixed_ref, before_ref, columns, member)
            conv_ref[:, columns] = conv
            gated_ref[:, columns] = (queries_ref[:, columns].astype(F32) * conv).astype(BF16)
        part_body(offsets, True, held_ref, gated_ref, *part_refs)

    for copy in copies:
        copy.wait()


def part_body(offsets, sibling, weight_ref, gated_ref, *refs):
    rows = gated_ref.shape[0]
    for k, offset in enumerate(offsets):
        width = refs[-1].shape[1]
        stacked = pl.ds(k * rows, rows)
        columns = block_columns(offset, sibling, width)
        part = jnp.dot(gated_ref[...], weight_ref[:, columns], preferred_element_type=F32)
        if sibling:
            refs[-1][stacked, :] = part.astype(BF16)
        else:
            summed = part.astype(BF16).astype(F32) + refs[0][stacked, :].astype(F32)
            refs[k - len(offsets)][...] = summed.astype(BF16)


def filter_grad_body(member, scale, doc_ref, grad_ref, mixed_ref, before_ref, out_ref, sums):
    taps, chan = grad_ref.shape
    groups = LANES // member
    here, before = [m.astype(F32) for m in row_masks(doc_ref, taps)]
    owner = lax.div(lax.broadcasted_iota(jnp.int32, (taps, LANES), 1), member)

    for tile in range(chan // LANES):
        columns = pl.ds(tile * LANES, LANES)
        both = jnp.concatenate([mixed_ref[:, columns], before_ref[:, columns]], axis=0)
        grad = grad_ref[:, columns]
        apart = jnp.concatenate([grad * (owner == g).astype(BF16) for g in range(groups)], axis=0)
        every = lax.dot_general(apart, both, NT, preferred_element_type=F32)
        for g in range(groups):
            one = every[g * taps : (g + 1) * taps]
            one = one[:, :taps] * here + one[:, taps:] * before
            total = one[:SUBLANES]
            for b in range(SUBLANES, taps, SUBLANES):
                total = total + pltpu.roll(one[b : b + SUBLANES], taps - b, 1)
            sums[tile * groups + g] = total

    total = sums[:, 0, :]
    for i in range(1, SUBLANES):
        total = total + pltpu.roll(sums[:, i, :], taps - i, 1)
    out_ref[...] = scale * jnp.dot(
        total, mirror(taps).astype(F32), precision=lax.Precision.HIGHEST, preferred_element_type=F32
    )


def own_and_filter_grad_body(body, offsets, weight_ref, gated_ref, came_ref, *refs):
    *operand_refs, held_ref, own_ref, terms_ref, sums = refs
    rows = own_ref.shape[0]
    last = came_ref.at[pl.ds(came_ref.shape[0] - rows, rows)]
    part_body(offsets, False, weight_ref, gated_ref, last, held_ref, own_ref)
    body(*operand_refs, terms_ref, sums)


def input_grads_body(member, band_ref, grad_ref, after_ref, keys_ref, values_ref, gated_ref, conv_ref, *refs):
    chan = grad_ref.shape[1]
    q_ref, k_ref, v_ref = refs
    for tile in range(chan // LANES):
        columns = pl.ds(tile * LANES, LANES)
        mixed_grad = filtered(band_ref, grad_ref, after_ref, columns, member)
        k_ref[:, columns] = (mixed_grad * values_ref[:, columns].astype(F32)).astype(BF16)
        v_ref[:, columns] = (mixed_grad * keys_ref[:, columns].astype(F32)).astype(BF16)
        q_ref[:, columns] = (gated_ref[:, columns] * conv_ref[:, columns]).astype(BF16)


def finish_body(count, *refs):
    *parts, out_ref, filter_ref = refs
    out_ref[...] = sum(ref[...].astype(F32) for ref in parts[count:]).astype(BF16)
    filter_ref[...] = sum(ref[...] for ref in parts[:count])


def shift(value, axis, by):
    devices = lax.axis_size(axis)
    return lax.ppermute(value, axis, [(i, i + by) for i in range(devices) if 0 <= i + by < devices])


def swap(value, mask):
    devices = lax.axis_size("tensor")
    return lax.ppermute(value, "tensor", [(i, i ^ mask) for i in range(devices)])


def turn(value, by):
    devices = lax.axis_size("dp")
    return lax.ppermute(value, "dp", [(i, (i + by) % devices) for i in range(devices)])


def on_device(queries, keys, values, doc_start, filters, out_weight, out_grad):
    rows, chan = queries.shape
    groups, taps = filters.shape
    member = chan // groups
    n = lax.axis_size("tensor")
    width = out_weight.shape[1] // n
    assert rows == taps == LANES and LANES % member == 0
    doc = doc_start.reshape(1, rows)
    tile, tile32, block = ((rows, chan), BF16), ((rows, chan), F32), ((rows, width), BF16)
    bands = pltpu.VMEM((groups * taps, 2 * taps), BF16)

    mixed = (keys.astype(F32) * values.astype(F32)).astype(BF16)
    before = shift(mixed, "dp", 1)
    staged = n == 8 and lax.axis_size("dp") == 4
    some, rest = (3, 1), (2, 0)
    if staged:
        at = lambda pairs: [block_columns(offset, sibling, width) for sibling, offsets in pairs for offset in offsets]
        blocks = functools.partial(at, ((True, some), (True, rest), (False, (3, 1, 2))))
        late = functools.partial(at, ((False, (0,)),))
        early_count, late_count = 7, 1
    else:
        early_count, late_count = 8, 0
        step = out_weight.shape[1] // early_count
        blocks, late = lambda: [pl.ds(k * step, step) for k in range(early_count)], lambda: []
    late_rows = max(late_count * width, LANES)
    fwd, bwd, total, late_grad, weight = pl.pallas_call(
        functools.partial(front_body, blocks, late, 7),
        out_shape=[bands, bands] + [jax.ShapeDtypeStruct(*s) for s in (((chan, rows), F32), ((late_rows, rows), BF16))]
        + [pltpu.VMEM(out_weight.shape, BF16)],
        in_specs=[pl.BlockSpec(memory_space=pltpu.HBM)] * 4,
        out_specs=[VMEM] * 5,
        scratch_shapes=[
            pltpu.VMEM(doc.shape, jnp.int32), pltpu.VMEM((groups, taps), F32), pltpu.VMEM((groups, taps), F32),
            pltpu.VMEM(out_grad.shape, BF16), pltpu.SemaphoreType.DMA((2,)),
            pltpu.SemaphoreType.DMA((early_count + late_count,)), pltpu.SemaphoreType.DMA((early_count,)),
        ],
        compiler_params=pltpu.CompilerParams(vmem_limit_bytes=16 * MIB),
        cost_estimate=cost(6.0),
        name="front",
    )(*(pltpu.with_memory_space_constraint(v, pltpu.HBM) for v in (doc, filters, out_grad, out_weight)))
    fwd, bwd = held_in_vmem(fwd), held_in_vmem(bwd)

    landed = [pltpu.SemaphoreType.DMA((max(1, late_count),))]
    finish_gated = functools.partial(gated_grad_body, late)
    if staged:
        stack = ((len(some + rest) * rows, width), BF16)
        weight, conv, gated, came = call(
            functools.partial(conv_body, member, some + rest, late), (out_weight, fwd, mixed, before, queries, weight),
            [tile32, tile, stack], "conv", 2.6, held=5, hbm=1, scratch=landed,
        )
        came = swap(came, 1)
        weight, gated_grad, conv_grad, leading = call(
            finish_gated, (doc, weight, total, late_grad, queries), [tile32, tile, tile], "gated_grad", 1.5, held=1
        )
        weight, far, near_x, near_y = call(
            functools.partial(part_body, (some + rest)[:3], False), (weight, gated, came), [block] * 3, "sums", 1.1, held=0
        )
        far, near_x, near_y = swap(far, 6), swap(near_x, 2), swap(near_y, 4)
    else:
        weight, conv, gated = call(
            functools.partial(conv_body, member, (), late), (out_weight, fwd, mixed, before, queries, weight),
            [tile32, tile], "conv", 1.2, held=5, hbm=1, scratch=landed,
        )
        weight, gated_grad, conv_grad, leading = call(
            finish_gated, (doc, weight, total, late_grad, queries), [tile32, tile, tile], "gated_grad", 1.5, held=1
        )
        partial_out = jnp.dot(gated, out_weight, preferred_element_type=F32).astype(BF16)
        output = lax.psum_scatter(partial_out, "tensor", scatter_dimension=1, tiled=True)
    after = shift(leading, "dp", -1)
    scale = (rows * lax.axis_size("dp") * member) ** (-0.5)
    body, operands = functools.partial(filter_grad_body, member, scale), (doc, conv_grad, mixed, before)
    scratch = [pltpu.VMEM((groups, SUBLANES, taps), F32)]
    if staged:
        weight, own, terms = call(
            functools.partial(own_and_filter_grad_body, body, rest[1:]), (weight, gated, came, *operands),
            [block, ((groups, taps), F32)], "filter_grad", 2.0, scratch=scratch, held=0,
        )
    else:
        (terms,) = call(body, operands, [((groups, taps), F32)], "filter_grad", 1.7, scratch=scratch)
    if staged:
        terms = terms + lax.ppermute(terms, "dp", [(i, i ^ 1) for i in range(4)])
        terms = (terms, turn(terms, 2))
    else:
        terms = (lax.psum(terms, "dp"),)
    q_grad, k_grad, v_grad = call(
        functools.partial(input_grads_body, member), (bwd, conv_grad, after, keys, values, gated_grad, conv),
        [tile, tile, tile], "input_grads", 2.0,
    )
    if staged:
        output, filter_grad = call(
            functools.partial(finish_body, len(terms)), (*terms, own, near_x, near_y, far),
            [block, ((groups, taps), F32)], "finish", 0.9,
        )
    else:
        filter_grad = sum(terms)
    return (output, q_grad, k_grad, v_grad, filter_grad)


def solution(mesh):
    split = P("dp", "tensor")
    return jax.shard_map(
        on_device,
        mesh=mesh,
        in_specs=(split, split, split, P("dp"), P("tensor", None), P("tensor", None), P("dp", None)),
        out_specs=(split, split, split, split, P("tensor", None)),
        check_vma=False,
    )
```

```python
import functools

import jax
import jax.numpy as jnp
from jax import lax
from jax.experimental import pallas as pl
from jax.experimental.pallas import tpu as pltpu
from jax.sharding import PartitionSpec as P

F32, BF16 = jnp.float32, jnp.bfloat16
LANES = 128
SUBLANES = 8
NT = (((1,), (1,)), ((), ()))
VMEM = pl.BlockSpec(memory_space=pltpu.VMEM)
MIB = 1 << 20


def cost(us):
    return pl.CostEstimate(flops=int(us * 1.1e9), bytes_accessed=int(us * 3.6e6), transcendentals=0)


def call(body, operands, outs, name, us, scratch=(), held=None, hbm=0):
    shapes = [jax.ShapeDtypeStruct(*s) for s in outs]
    operands, aliases = list(operands), {}
    for k in range(hbm):
        operands[k] = pltpu.with_memory_space_constraint(operands[k], pltpu.HBM)
    if held is not None:
        operands[held] = held_in_vmem(operands[held])
        shapes = [pltpu.VMEM(operands[held].shape, operands[held].dtype)] + shapes
        aliases = {held: 0}
    return pl.pallas_call(
        body,
        out_shape=shapes,
        in_specs=[pl.BlockSpec(memory_space=pltpu.HBM)] * hbm + [VMEM] * (len(operands) - hbm),
        out_specs=[VMEM] * len(shapes),
        input_output_aliases=aliases,
        scratch_shapes=list(scratch),
        compiler_params=pltpu.CompilerParams(vmem_limit_bytes=16 * MIB),
        cost_estimate=cost(us),
        name=name,
    )(*operands)


def held_in_vmem(value):
    return pltpu.with_memory_space_constraint(value, pltpu.VMEM)


def apart(body):
    pl.when(lax.axis_index("dp") >= 0)(body)


def mirror(taps):
    i = lax.broadcasted_iota(jnp.int32, (taps, taps), 0)
    j = lax.broadcasted_iota(jnp.int32, (taps, taps), 1)
    return (i + j == taps) | ((i == 0) & (j == 0))


def doc_offsets(doc_ref, taps):
    first = lax.axis_index("dp") * taps
    lane = jnp.broadcast_to((doc_ref[...] - first).astype(F32), (taps, taps))
    return lane, lane.T


def grid_of(taps):
    return (
        lax.broadcasted_iota(jnp.int32, (taps, taps), 0).astype(F32),
        lax.broadcasted_iota(jnp.int32, (taps, taps), 1).astype(F32),
    )


def row_masks(doc_ref, taps):
    _, doc = doc_offsets(doc_ref, taps)
    t, s = grid_of(taps)
    return (s <= t) & (s >= doc), (s > t) & (s - taps >= doc)


def column_masks(doc_ref, taps):
    doc, _ = doc_offsets(doc_ref, taps)
    s, t = grid_of(taps)
    return (s <= t) & (s >= doc), (s > t) & (s >= doc[:, taps - 1 :])


def front_body(blocks, late, ahead, doc_hbm, filt_hbm, grad_hbm, weight_hbm, fwd_ref, bwd_ref, total_ref, late_ref,
               weight_ref, doc_ref, filt_ref, turned, grad_ref, came, arrived, landed):
    groups, taps = filt_ref.shape
    blocks, late = blocks(), late()
    count = len(blocks)
    share = -(-groups // max(1, count - 1))
    small = [
        pltpu.make_async_copy(src, dst, came.at[k])
        for k, (src, dst) in enumerate(((doc_hbm, doc_ref), (filt_hbm, filt_ref)))
    ]
    grads = [
        pltpu.make_async_copy(grad_hbm.at[:, b], grad_ref.at[:, b], arrived.at[k]) for k, b in enumerate(blocks + late)
    ]
    weights = [
        pltpu.make_async_copy(weight_hbm.at[:, b], weight_ref.at[:, b], landed.at[k]) for k, b in enumerate(blocks)
    ]
    for copy in small + grads[:1] + weights[:1] + grads[1:] + weights[1:ahead]:
        copy.start()
    small[0].wait()
    here, before = [m.astype(BF16) for m in row_masks(doc_ref, taps)]
    here_t, after = [m.astype(BF16) for m in column_masks(doc_ref, taps)]
    small[1].wait()
    turned[...] = jnp.dot(filt_ref[...].astype(BF16), mirror(taps).astype(BF16), preferred_element_type=F32)

    def circulant(ref, g):
        line = jnp.broadcast_to(ref[pl.ds(g, 1), :], (taps, taps))
        return pltpu.roll(line, 0, 1, stride=1, stride_axis=0).astype(BF16)

    def bands(start, stop):
        for g in range(start, min(groups, stop)):
            rows = pl.ds(g * taps, taps)
            fwd = circulant(turned, g)
            fwd_ref[rows, :taps] = fwd * here
            fwd_ref[rows, taps:] = fwd * before
            bwd = circulant(filt_ref, g)
            bwd_ref[rows, :taps] = bwd * here_t
            bwd_ref[rows, taps:] = bwd * after

    for k, columns in enumerate(blocks):
        grads[k].wait()
        weights[k].wait()
        if k + ahead < count:
            weights[k + ahead].start()

        @apart
        def _():
            part = jnp.dot(weight_ref[:, columns], grad_ref[:, columns].T, preferred_element_type=F32)
            total_ref[...] = part if k == 0 else total_ref[...] + part
            bands(k * share, (k + 1) * share)

    for k, columns in enumerate(late):
        grads[count + k].wait()
        width = columns.size
        late_ref[pl.ds(k * width, width), :] = grad_ref[:, columns].T


def gated_grad_body(late, doc_ref, weight_ref, total_ref, late_ref, queries_ref, held_ref, gated_ref, conv_ref, lead_ref):
    del held_ref
    taps = doc_ref.shape[1]
    total = total_ref[...]
    for k, columns in enumerate(late()):
        width = columns.size
        total = total + jnp.dot(weight_ref[:, columns], late_ref[pl.ds(k * width, width), :], preferred_element_type=F32)
    total = total.T
    gated_ref[...] = total
    conv_grad = (total * queries_ref[...].astype(F32)).astype(BF16)
    conv_ref[...] = conv_grad
    _, doc = doc_offsets(doc_ref, taps)
    lead_ref[...] = jnp.where(doc[:, :1] < 0, conv_grad, jnp.zeros_like(conv_grad))


def filtered(band_ref, near_ref, far_ref, columns, member):
    taps = near_ref.shape[0]
    groups = LANES // member
    both = jnp.concatenate([near_ref[:, columns], far_ref[:, columns]], axis=0)
    bands = pl.ds(columns.start // LANES * groups * taps, groups * taps)
    every = jnp.dot(band_ref[bands, :], both, preferred_element_type=F32)
    owner = lax.div(lax.broadcasted_iota(jnp.int32, (taps, LANES), 1), member)
    total = every[:taps]
    for g in range(1, groups):
        total = jnp.where(owner == g, every[g * taps : (g + 1) * taps], total)
    return total


def block_columns(offset, sibling, width):
    me = lax.axis_index("tensor")
    chip, core = lax.div(me, 2), lax.rem(me, 2)
    owner = 2 * jnp.bitwise_xor(chip, offset) + (1 - core if sibling else core)
    return pl.ds(pl.multiple_of(owner * width, width), width)


def conv_body(member, offsets, late, weight_hbm, band_ref, mixed_ref, before_ref, queries_ref, weight_ref, held_ref, conv_ref, gated_ref, *refs):
    *part_refs, landed = refs
    copies = [pltpu.make_async_copy(weight_hbm.at[:, b], held_ref.at[:, b], landed.at[k]) for k, b in enumerate(late())]
    for copy in copies:
        copy.start()

    @apart
    def _():
        for tile in range(mixed_ref.shape[1] // LANES):
            columns = pl.ds(tile * LANES, LANES)
            conv = filtered(band_ref, mixed_ref, before_ref, columns, member)
            conv_ref[:, columns] = conv
            gated_ref[:, columns] = (queries_ref[:, columns].astype(F32) * conv).astype(BF16)
        part_body(offsets, True, held_ref, gated_ref, *part_refs)

    for copy in copies:
        copy.wait()


def part_body(offsets, sibling, weight_ref, gated_ref, *refs):
    rows = gated_ref.shape[0]
    for k, offset in enumerate(offsets):
        width = refs[-1].shape[1]
        stacked = pl.ds(k * rows, rows)
        columns = block_columns(offset, sibling, width)
        part = jnp.dot(gated_ref[...], weight_ref[:, columns], preferred_element_type=F32)
        if sibling:
            refs[-1][stacked, :] = part.astype(BF16)
        else:
            summed = part + refs[0][stacked, :].astype(F32)
            refs[k - len(offsets)][...] = summed.astype(BF16)


def filter_grad_body(member, scale, doc_ref, grad_ref, mixed_ref, before_ref, out_ref, sums):
    taps, chan = grad_ref.shape
    groups = LANES // member
    here, before = [m.astype(F32) for m in row_masks(doc_ref, taps)]
    owner = lax.div(lax.broadcasted_iota(jnp.int32, (taps, LANES), 1), member)

    for tile in range(chan // LANES):
        columns = pl.ds(tile * LANES, LANES)
        both = jnp.concatenate([mixed_ref[:, columns], before_ref[:, columns]], axis=0)
        grad = grad_ref[:, columns]
        apart = jnp.concatenate([grad * (owner == g).astype(BF16) for g in range(groups)], axis=0)
        every = lax.dot_general(apart, both, NT, preferred_element_type=F32)
        for g in range(groups):
            one = every[g * taps : (g + 1) * taps]
            one = one[:, :taps] * here + one[:, taps:] * before
            total = one[:SUBLANES]
            for b in range(SUBLANES, taps, SUBLANES):
                total = total + pltpu.roll(one[b : b + SUBLANES], taps - b, 1)
            sums[tile * groups + g] = total

    total = sums[:, 0, :]
    for i in range(1, SUBLANES):
        total = total + pltpu.roll(sums[:, i, :], taps - i, 1)
    out_ref[...] = scale * jnp.dot(
        total, mirror(taps).astype(F32), precision=lax.Precision.HIGHEST, preferred_element_type=F32
    )


def own_and_filter_grad_body(body, offsets, weight_ref, gated_ref, came_ref, *refs):
    *operand_refs, held_ref, own_ref, terms_ref, sums = refs
    rows = own_ref.shape[0]
    last = came_ref.at[pl.ds(came_ref.shape[0] - rows, rows)]
    part_body(offsets, False, weight_ref, gated_ref, last, held_ref, own_ref)
    body(*operand_refs, terms_ref, sums)


def input_grads_body(member, band_ref, grad_ref, after_ref, keys_ref, values_ref, gated_ref, conv_ref, *refs):
    chan = grad_ref.shape[1]
    q_ref, k_ref, v_ref = refs
    for tile in range(chan // LANES):
        columns = pl.ds(tile * LANES, LANES)
        mixed_grad = filtered(band_ref, grad_ref, after_ref, columns, member)
        k_ref[:, columns] = (mixed_grad * values_ref[:, columns].astype(F32)).astype(BF16)
        v_ref[:, columns] = (mixed_grad * keys_ref[:, columns].astype(F32)).astype(BF16)
        q_ref[:, columns] = (gated_ref[:, columns] * conv_ref[:, columns]).astype(BF16)


def finish_body(count, *refs):
    *parts, out_ref, filter_ref = refs
    out_ref[...] = sum(ref[...].astype(F32) for ref in parts[count:]).astype(BF16)
    filter_ref[...] = sum(ref[...] for ref in parts[:count])


def shift(value, axis, by):
    devices = lax.axis_size(axis)
    return lax.ppermute(value, axis, [(i, i + by) for i in range(devices) if 0 <= i + by < devices])


def swap(value, mask):
    devices = lax.axis_size("tensor")
    return lax.ppermute(value, "tensor", [(i, i ^ mask) for i in range(devices)])


def turn(value, by):
    devices = lax.axis_size("dp")
    return lax.ppermute(value, "dp", [(i, (i + by) % devices) for i in range(devices)])


def on_device(queries, keys, values, doc_start, filters, out_weight, out_grad):
    rows, chan = queries.shape
    groups, taps = filters.shape
    member = chan // groups
    n = lax.axis_size("tensor")
    width = out_weight.shape[1] // n
    assert rows == taps == LANES and LANES % member == 0
    doc = doc_start.reshape(1, rows)
    tile, tile32, block = ((rows, chan), BF16), ((rows, chan), F32), ((rows, width), BF16)
    bands = pltpu.VMEM((groups * taps, 2 * taps), BF16)

    mixed = (keys.astype(F32) * values.astype(F32)).astype(BF16)
    before = shift(mixed, "dp", 1)
    staged = n == 8 and lax.axis_size("dp") == 4
    some, rest = (3, 1), (2, 0)
    if staged:
        at = lambda pairs: [block_columns(offset, sibling, width) for sibling, offsets in pairs for offset in offsets]
        blocks = functools.partial(at, ((True, some), (True, rest), (False, (3, 1, 2))))
        late = functools.partial(at, ((False, (0,)),))
        early_count, late_count = 7, 1
    else:
        early_count, late_count = 8, 0
        step = out_weight.shape[1] // early_count
        blocks, late = lambda: [pl.ds(k * step, step) for k in range(early_count)], lambda: []
    late_rows = max(late_count * width, LANES)
    fwd, bwd, total, late_grad, weight = pl.pallas_call(
        functools.partial(front_body, blocks, late, 7),
        out_shape=[bands, bands] + [jax.ShapeDtypeStruct(*s) for s in (((chan, rows), F32), ((late_rows, rows), BF16))]
        + [pltpu.VMEM(out_weight.shape, BF16)],
        in_specs=[pl.BlockSpec(memory_space=pltpu.HBM)] * 4,
        out_specs=[VMEM] * 5,
        scratch_shapes=[
            pltpu.VMEM(doc.shape, jnp.int32), pltpu.VMEM((groups, taps), F32), pltpu.VMEM((groups, taps), F32),
            pltpu.VMEM(out_grad.shape, BF16), pltpu.SemaphoreType.DMA((2,)),
            pltpu.SemaphoreType.DMA((early_count + late_count,)), pltpu.SemaphoreType.DMA((early_count,)),
        ],
        compiler_params=pltpu.CompilerParams(vmem_limit_bytes=16 * MIB),
        cost_estimate=cost(6.0),
        name="front",
    )(*(pltpu.with_memory_space_constraint(v, pltpu.HBM) for v in (doc, filters, out_grad, out_weight)))
    fwd, bwd = held_in_vmem(fwd), held_in_vmem(bwd)

    landed = [pltpu.SemaphoreType.DMA((max(1, late_count),))]
    finish_gated = functools.partial(gated_grad_body, late)
    if staged:
        stack = ((len(some + rest) * rows, width), BF16)
        weight, conv, gated, came = call(
            functools.partial(conv_body, member, some + rest, late), (out_weight, fwd, mixed, before, queries, weight),
            [tile32, tile, stack], "conv", 2.6, held=5, hbm=1, scratch=landed,
        )
        came = swap(came, 1)
        weight, gated_grad, conv_grad, leading = call(
            finish_gated, (doc, weight, total, late_grad, queries), [tile32, tile, tile], "gated_grad", 1.5, held=1
        )
        weight, far, near_x, near_y = call(
            functools.partial(part_body, (some + rest)[:3], False), (weight, gated, came), [block] * 3, "sums", 1.1, held=0
        )
        far, near_x, near_y = swap(far, 6), swap(near_x, 2), swap(near_y, 4)
    else:
        weight, conv, gated = call(
            functools.partial(conv_body, member, (), late), (out_weight, fwd, mixed, before, queries, weight),
            [tile32, tile], "conv", 1.2, held=5, hbm=1, scratch=landed,
        )
        weight, gated_grad, conv_grad, leading = call(
            finish_gated, (doc, weight, total, late_grad, queries), [tile32, tile, tile], "gated_grad", 1.5, held=1
        )
        partial_out = jnp.dot(gated, out_weight, preferred_element_type=F32).astype(BF16)
        output = lax.psum_scatter(partial_out, "tensor", scatter_dimension=1, tiled=True)
    after = shift(leading, "dp", -1)
    scale = (rows * lax.axis_size("dp") * member) ** (-0.5)
    body, operands = functools.partial(filter_grad_body, member, scale), (doc, conv_grad, mixed, before)
    scratch = [pltpu.VMEM((groups, SUBLANES, taps), F32)]
    if staged:
        weight, own, terms = call(
            functools.partial(own_and_filter_grad_body, body, rest[1:]), (weight, gated, came, *operands),
            [block, ((groups, taps), F32)], "filter_grad", 2.0, scratch=scratch, held=0,
        )
    else:
        (terms,) = call(body, operands, [((groups, taps), F32)], "filter_grad", 1.7, scratch=scratch)
    if staged:
        terms = terms + lax.ppermute(terms, "dp", [(i, i ^ 1) for i in range(4)])
        terms = (terms, turn(terms, 2))
    else:
        terms = (lax.psum(terms, "dp"),)
    q_grad, k_grad, v_grad = call(
        functools.partial(input_grads_body, member), (bwd, conv_grad, after, keys, values, gated_grad, conv),
        [tile, tile, tile], "input_grads", 2.0,
    )
    if staged:
        output, filter_grad = call(
            functools.partial(finish_body, len(terms)), (*terms, own, near_x, near_y, far),
            [block, ((groups, taps), F32)], "finish", 0.9,
        )
    else:
        filter_grad = sum(terms)
    return (output, q_grad, k_grad, v_grad, filter_grad)


def solution(mesh):
    split = P("dp", "tensor")
    return jax.shard_map(
        on_device,
        mesh=mesh,
        in_specs=(split, split, split, P("dp"), P("tensor", None), P("tensor", None), P("dp", None)),
        out_specs=(split, split, split, split, P("tensor", None)),
        check_vma=False,
    )
```
